256 devices in a mesh: band: 128 (over z_hi, y, x, core), head: 2 (over z_lo).
Axes of the slice: x: 4, y: 4, z: 8 (z_hi: 4, z_lo: 2; z = z_hi * 2 + z_lo), core: 2. Of those that a mesh axis runs over, the one named last changes fastest.
Arguments:
- queries: bfloat16 [128, 3, 128, 512], P('band', None, None, 'head'), may hold values from -16 to 16
- attn_keys: bfloat16 [128, 3, 128, 512], P('band', None, None, 'head'), may hold values from -16 to 16
- attn_values: bfloat16 [128, 3, 128, 512], P('band', None, None, 'head'), may hold values from -16 to 16
- out_proj: bfloat16 [512, 1024], P('head'), may hold values from -0.25 to 0.25
- grad_out: bfloat16 [128, 3, 128, 1024], P('band', None, 'head'), may hold values from -24 to 24
- plane_axes: int32 [3, 2], replicated, may hold values from 0 to 2, as said below
Outputs:
- layer_out: bfloat16 [128, 3, 128, 1024], P('band', None, 'head')
- grad_queries: bfloat16 [128, 3, 128, 512], P('band', None, None, 'head')
- grad_keys: bfloat16 [128, 3, 128, 512], P('band', None, None, 'head')
- grad_values: bfloat16 [128, 3, 128, 512], P('band', None, None, 'head')
The draws below stay inside these ranges and needn't reach their ends.
Inputs may be any that keep to these rules, and one draw needn't show every extreme that they name: `plane_axes`: row p holds plane p's row axis and then its column axis, two different world axes; the three planes lack three different world axes.
All inputs are finite; a program needn't handle non-finite values.
Results may differ from the reference program's by a relative error of at most 0.018.
Values may be sent and summed in bfloat16 or wider, within the bound.
No kernel may reach another device: no remote copies, remote signals or barrier semaphores. Data moves between devices by JAX's collectives and lax.ppermute only.
A program may use at most 64 MiB of HBM per device.

```python
import jax
import jax.numpy as jnp
from jax import lax

HEADS = 8
HEAD_DIM = 64
D = 1024
R = 128
HF = 512


def query_key_pair(base_key):
    mixed = jax.random.fold_in(base_key, 4242)
    subkeys = jax.random.split(mixed, 4)
    width = HEADS * HEAD_DIM
    shape = (R, 3, R, width)
    queries = jnp.clip(jax.random.normal(subkeys[2], shape, jnp.float32), -6.0, 6.0)
    keys_out = jnp.clip(jax.random.normal(subkeys[3], shape, jnp.float32), -6.0, 6.0)
    return (queries, keys_out)


def draw_queries(key, part):
    return query_key_pair(key)[0].astype(jnp.bfloat16)


def draw_attn_keys(key, part):
    return query_key_pair(key)[1].astype(jnp.bfloat16)


def draw_plane_axes(key, part):
    mixed = jax.random.fold_in(key, 77)
    subkeys = jax.random.split(mixed, 2)
    missing = jax.random.permutation(subkeys[0], 3).astype(jnp.int32)
    flipped = jax.random.randint(subkeys[1], (3,), 0, 2)
    first = (missing + 1) % 3
    second = (missing + 2) % 3
    row_axis = jnp.where(flipped == 1, second, first)
    column_axis = jnp.where(flipped == 1, first, second)
    return jnp.stack([row_axis, column_axis], axis=1).astype(jnp.int32)


def block_levels(own_key, dims, shards, smallest, top_value):
    factor_of, own = 1.0, jax.random.fold_in(own_key, 6)
    for position, parts in shards:
        heights = jnp.exp(jax.random.uniform(jax.random.fold_in(own, position), (parts,), jnp.float32, smallest / len(shards), top_value / len(shards)))
        factor_of = factor_of * jnp.repeat(heights, dims[position] // parts).reshape([-1 if axis == position else 1 for axis in range(len(dims))])
    return factor_of


def centred(stream_key, dims, deviation, bound, cuts=(), kind=jnp.bfloat16):
    gain = block_levels(stream_key, dims, cuts, -0.22, 0.18) if cuts else 1.0
    result = jax.random.normal(stream_key, dims, jnp.float32) * deviation * gain
    return jnp.minimum(jnp.maximum(result, -bound), bound).astype(kind)


def setup_inputs(seed: int = 0) -> dict:
    streams_of = jax.random.split(jax.random.key(seed), 7)
    queries = draw_queries(jax.random.fold_in(streams_of[6], 71), 0)
    attn_keys = draw_attn_keys(jax.random.fold_in(streams_of[6], 71), 0)
    attn_values = centred(streams_of[2], (R, 3, R, HF), 3.0, 16.0, ((0, 128), (3, 2)))
    out_proj = centred(streams_of[3], (HF, D), HF ** -0.5, 0.25, ((0, 2),))
    grad_out = centred(streams_of[4], (R, 3, R, D), 4.0, 24.0, ((0, 128), (2, 2)))
    plane_axes = draw_plane_axes(jax.random.fold_in(streams_of[6], 71), 0)
    return {"queries": queries, "attn_keys": attn_keys, "attn_values": attn_values, "out_proj": out_proj, "grad_out": grad_out, "plane_axes": plane_axes}


def partner_blocks(plane_axes):
    axis_of = jnp.concatenate([plane_axes[:, 0], plane_axes[:, 1]]).astype(jnp.int32)
    blocks = jnp.arange(6, dtype=jnp.int32)
    same = (axis_of[:, None] == axis_of[None, :]) & (blocks[:, None] != blocks[None, :])
    return jnp.sum(jnp.where(same, blocks[None, :], 0), axis=1).astype(jnp.int32)


def by_head(values):
    return values.reshape(values.shape[:-1] + (values.shape[-1] // HEAD_DIM, HEAD_DIM))


def flatten(values):
    return values.reshape(values.shape[:2] + (-1,))


def log_total(scores):
    top = jnp.max(scores, axis=-1, keepdims=True)
    return top[..., 0] + jnp.log(jnp.sum(jnp.exp(scores - top), axis=-1))


def line_scores(query_line, key_line, partner):
    factor = HEAD_DIM ** -0.5
    query_heads = by_head(query_line).astype(jnp.float32)
    key_heads = by_head(key_line).astype(jnp.float32)
    partner_keys = jnp.take(key_heads, partner, axis=0)
    cross = jnp.einsum("bahe,bche->bhac", query_heads, partner_keys) * factor
    own = jnp.einsum("bahe,bche->bhac", query_heads[:3], key_heads[:3]) * factor
    return own, cross


def forward_core(own, cross, value_line, partner):
    value_heads = by_head(value_line).astype(jnp.float32)
    partner_values = jnp.take(value_heads, partner, axis=0)
    length = own.shape[-1]
    near_scores = jnp.concatenate([own, cross[:3]], axis=-1)
    near_total = log_total(near_scores)
    near_prob = jnp.exp(near_scores - near_total[..., None]).astype(jnp.bfloat16).astype(jnp.float32)
    near_out = jnp.einsum("bhac,bche->bahe", near_prob[..., :length], value_heads[:3])
    near_out = near_out + jnp.einsum("bhac,bche->bahe", near_prob[..., length:], partner_values[:3])
    far_total = log_total(cross[3:])
    far_prob = jnp.exp(cross[3:] - far_total[..., None]).astype(jnp.bfloat16).astype(jnp.float32)
    far_out = jnp.einsum("bhac,bche->bahe", far_prob, partner_values[3:])
    return (jnp.transpose(near_total, (0, 2, 1)), flatten(near_out),
            jnp.transpose(far_total, (0, 2, 1)), flatten(far_out))


def backward_core(own, cross, line, partner):
    factor = HEAD_DIM ** -0.5
    query_line, key_line, value_line, grad_line, total_line, delta_line = line
    query_heads = by_head(query_line).astype(jnp.float32)
    key_heads = by_head(key_line).astype(jnp.float32)
    value_heads = by_head(value_line).astype(jnp.float32)
    grad_heads = by_head(grad_line).astype(jnp.float32)
    partner_keys = jnp.take(key_heads, partner, axis=0)
    partner_values = jnp.take(value_heads, partner, axis=0)
    total = jnp.transpose(total_line, (0, 2, 1))[..., None]
    delta = jnp.transpose(delta_line, (0, 2, 1))[..., None]
    cross_prob = jnp.exp(cross - total).astype(jnp.bfloat16).astype(jnp.float32)
    own_prob = jnp.exp(own - total[:3]).astype(jnp.bfloat16).astype(jnp.float32)
    cross_grad = jnp.einsum("bahe,bche->bhac", grad_heads, partner_values)
    own_grad = jnp.einsum("bahe,bche->bhac", grad_heads[:3], value_heads[:3])
    cross_step = (cross_prob * (cross_grad - delta) * factor).astype(jnp.bfloat16).astype(jnp.float32)
    own_step = (own_prob * (own_grad - delta[:3]) * factor).astype(jnp.bfloat16).astype(jnp.float32)
    grad_query = jnp.einsum("bhac,bche->bahe", cross_step, partner_keys)
    grad_query = grad_query.at[:3].add(jnp.einsum("bhac,bche->bahe", own_step, key_heads[:3]))
    toward_keys = jnp.einsum("bhac,bahe->bche", cross_step, query_heads)
    toward_values = jnp.einsum("bhac,bahe->bche", cross_prob, grad_heads)
    grad_key = jnp.take(toward_keys, partner, axis=0)
    grad_key = grad_key.at[:3].add(jnp.einsum("bhac,bahe->bche", own_step, query_heads[:3]))
    grad_value = jnp.take(toward_values, partner, axis=0)
    grad_value = grad_value.at[:3].add(jnp.einsum("bhac,bahe->bche", own_prob, grad_heads[:3]))
    return flatten(grad_query), flatten(grad_key), flatten(grad_value)


def to_lines(values):
    return jnp.concatenate([values, jnp.transpose(values, (2, 1, 0, 3))], axis=1)


def from_lines(values):
    return values[:, :3] + jnp.transpose(values[:, 3:], (2, 1, 0, 3))


def reference(queries, attn_keys, attn_values, out_proj, grad_out, plane_axes):
    partner = partner_blocks(plane_axes)
    query_lines = to_lines(queries)
    key_lines = to_lines(attn_keys)
    value_lines = to_lines(attn_values)

    def forward_one(line):
        own, cross = line_scores(line[0], line[1], partner)
        return forward_core(own, cross, line[2], partner)

    near_total, near_out, far_total, far_out = lax.map(forward_one, (query_lines, key_lines, value_lines))
    far_total = jnp.transpose(far_total, (2, 1, 0, 3))
    far_out = jnp.transpose(far_out, (2, 1, 0, 3))
    top = jnp.maximum(near_total, far_total)
    log_all = top + jnp.log(jnp.exp(near_total - top) + jnp.exp(far_total - top))
    attended = (by_head(near_out) * jnp.exp(near_total - log_all)[..., None]
                + by_head(far_out) * jnp.exp(far_total - log_all)[..., None])
    attended = attended.reshape(queries.shape).astype(jnp.bfloat16)
    layer_out = jnp.dot(attended.reshape(-1, HF), out_proj, preferred_element_type=jnp.float32)
    layer_out = layer_out.astype(jnp.bfloat16).reshape(R, 3, R, D)
    grad_attended = jnp.dot(grad_out.reshape(-1, D), out_proj.T, preferred_element_type=jnp.float32)
    grad_attended = grad_attended.astype(jnp.bfloat16).reshape(R, 3, R, HF)
    delta = jnp.sum(by_head(grad_attended).astype(jnp.float32) * by_head(attended).astype(jnp.float32), axis=-1)

    def backward_one(line):
        own, cross = line_scores(line[0], line[1], partner)
        return backward_core(own, cross, line, partner)

    grad_q, grad_k, grad_v = lax.map(backward_one, (query_lines, key_lines, value_lines, to_lines(grad_attended), to_lines(log_all), to_lines(delta)))
    return (layer_out, from_lines(grad_q).astype(jnp.bfloat16),
            from_lines(grad_k).astype(jnp.bfloat16), from_lines(grad_v).astype(jnp.bfloat16))
```

```python
import jax
import jax.numpy as jnp
from jax import lax
from jax.experimental import pallas as pl
from jax.experimental.pallas import tpu as pltpu
from jax.sharding import PartitionSpec as P

BF = jnp.bfloat16
F32 = jnp.float32
N = 128
HALF = 64
SENT = 18
MIXED = 14
FACTOR = 0.125
PARAMS = pltpu.CompilerParams(vmem_limit_bytes=48 * 1024 * 1024)
VMEM = pl.BlockSpec(memory_space=pltpu.VMEM)
SMEM = pl.BlockSpec(memory_space=pltpu.SMEM)


def nt(a, b):
    return lax.dot_general(a, b, (((1,), (1,)), ((), ())), preferred_element_type=F32)


def tn(a, b):
    return lax.dot_general(a, b, (((0,), (0,)), ((), ())), preferred_element_type=F32)


def nn(a, b):
    return lax.dot_general(a, b, (((1,), (0,)), ((), ())), preferred_element_type=F32)


def lane_masks():
    lane = lax.broadcasted_iota(jnp.int32, (N, N), 1)
    first = jnp.where(lane < HALF, 1.0, 0.0)
    return first.astype(BF), (1.0 - first).astype(BF)


def stack(x, masks):
    return jnp.concatenate([x * masks[0], x * masks[1]], axis=0)


def head_sums(product):
    row = lax.broadcasted_iota(jnp.int32, (8, 256), 0)
    lane = lax.broadcasted_iota(jnp.int32, (8, 256), 1)
    pick = jnp.where(lane // HALF == row, 1.0, 0.0).astype(BF)
    high = product.astype(BF)
    low = (product - high.astype(F32)).astype(BF)
    return nt(pick, high) + nt(pick, low)


def partners(axes_ref):
    axis = [axes_ref[b % 3, b // 3] for b in range(6)]
    found = []
    for b in range(6):
        other = jnp.int32(0)
        for c in range(6):
            if c != b:
                other = other + jnp.where(axis[c] == axis[b], jnp.int32(c), jnp.int32(0))
        found.append(other)
    return found


def pack_lines_kernel(q_ref, k_ref, v_ref, out_ref, stage):
    for a, ref in enumerate((q_ref, k_ref, v_ref)):
        for p in range(3):
            for g in range(2):
                rows = pl.ds(2 * (3 * a + p) + g, N, stride=SENT)
                stage[rows, :] = ref[p, :, N * g : N * g + N].astype(F32)
    out_ref[...] = stage[...].astype(BF)


def cotangent_kernel(own_ref, other_ref, proj_ref, out_ref):
    me = lax.axis_index("head")
    for ref, side in ((own_ref, me), (other_ref, 1 - me)):
        made = nt(ref[...], proj_ref[...]).astype(BF)
        for p in range(3):
            out_ref[p, pl.ds(pl.multiple_of(side * HALF, HALF), HALF), :] = made[
                HALF * p : HALF * p + HALF
            ]


def forward_kernel(
    axes_ref, q_ref, k_ref, v_ref, ga_ref, got_ref,
    send_ref, q6, k6, v6, near_ref, far_ref, totals_ref,
    stage, parts,
):
    partner = partners(axes_ref)
    masks = lane_masks()
    stage[...] = got_ref[...].astype(F32)
    for a, (mine, six) in enumerate(((q_ref, q6), (k_ref, k6), (v_ref, v6))):
        for p in range(3):
            six[p] = mine[p]
            for g in range(2):
                rows = pl.ds(2 * (3 * a + p) + g, N, stride=SENT)
                six[3 + p, :, N * g : N * g + N] = stage[rows, :].astype(BF)
    for b in range(6):
        for g in range(2):
            lanes = slice(N * g, N * g + N)
            queries = stack(q6[b, :, lanes] * BF(FACTOR), masks)
            scores = [nt(k6[partner[b], :, lanes], queries)]
            values = [v6[partner[b], :, lanes]]
            if b < 3:
                scores.append(nt(k6[b, :, lanes], queries))
                values.append(v6[b, :, lanes])
            top = jnp.max(scores[0], axis=0, keepdims=True)
            for s in scores[1:]:
                top = jnp.maximum(top, jnp.max(s, axis=0, keepdims=True))
            raised = [jnp.exp(s - top) for s in scores]
            total = jnp.sum(raised[0], axis=0, keepdims=True)
            for e in raised[1:]:
                total = total + jnp.sum(e, axis=0, keepdims=True)
            scale = 1.0 / total
            total = top + jnp.log(total)
            out = None
            for e, v in zip(raised, values):
                prob = (e * scale).astype(BF)
                both = jnp.concatenate([prob[:, :N], prob[:, N:]], axis=0)
                term = tn(both, stack(v, masks))
                out = term if out is None else out + term
            row = (0 if b < 3 else 24) + 4 * (b % 3) + 2 * g
            totals_ref[row : row + 1, :] = total[:, :N]
            totals_ref[row + 1 : row + 2, :] = total[:, N:]
            if b < 3:
                near_ref[b, :, lanes] = out
            else:
                far_ref[b - 3, :, lanes] = out.astype(BF)
    for p in range(3):
        totals_ref[12 + 4 * p : 16 + 4 * p, :] = head_sums(
            ga_ref[p].astype(F32) * near_ref[p]
        )[:4]
    totals_ref[36:40, :] = jnp.zeros((4, N), F32)
    parts[...] = jnp.zeros((N, N), F32)
    left = totals_ref[...]
    for piece in range(3):
        rounded = left.astype(BF).astype(F32)
        parts[40 * piece : 40 * piece + 40, :] = rounded
        left = left - rounded
    stage[pl.ds(12, N, stride=MIXED), :] = jnp.transpose(parts[...])
    stage[pl.ds(13, N, stride=MIXED), :] = jnp.zeros((N, N), F32)
    for p in range(3):
        for g in range(2):
            lanes = slice(N * g, N * g + N)
            stage[pl.ds(2 * p + g, N, stride=MIXED), :] = far_ref[p, :, lanes].astype(F32)
            stage[pl.ds(6 + 2 * p + g, N, stride=MIXED), :] = ga_ref[p, :, lanes].astype(F32)
    send_ref[...] = stage[: MIXED * N, :].astype(BF)


def both_totals(near, far):
    top = jnp.maximum(near, far)
    log_all = top + jnp.log(jnp.exp(near - top) + jnp.exp(far - top))
    return log_all, jnp.exp(near - log_all), jnp.exp(far - log_all)


def backward_kernel(
    axes_ref, q6, k6, v6, ga_ref, near_ref, far_ref, totals_ref, got_ref,
    att_ref, dq_ref, dk_ref, dv_ref, send_ref,
    stage, parts, ga6, log_all_ref, delta_ref, dk6, dv6,
):
    partner = partners(axes_ref)
    masks = lane_masks()
    stage[: MIXED * N, :] = got_ref[...].astype(F32)
    parts[...] = jnp.transpose(stage[pl.ds(12, N, stride=MIXED), :])
    arrived = parts[0:40, :] + (parts[40:80, :] + parts[80:120, :])
    for p in range(3):
        ga6[p] = ga_ref[p]
        for g in range(2):
            ga6[3 + p, :, N * g : N * g + N] = stage[
                pl.ds(6 + 2 * p + g, N, stride=MIXED), :
            ].astype(BF)
    row_log, row_near, row_far = both_totals(totals_ref[0:12, :], arrived[24:36])
    col_log, col_near, col_far = both_totals(arrived[0:12], totals_ref[24:36, :])
    log_all_ref[0:12, :] = row_log
    log_all_ref[12:24, :] = col_log
    row_delta = row_near * totals_ref[12:24, :]
    col_delta = col_near * arrived[12:24]
    for p in range(3):
        far_row = jnp.concatenate(
            [stage[pl.ds(2 * p + g, N, stride=MIXED), :] for g in range(2)], axis=1
        )
        heads = slice(4 * p, 4 * p + 4)
        delta_ref[4 * p : 4 * p + 4, :] = (
            row_delta[heads] + row_far[heads] * head_sums(ga_ref[p].astype(F32) * far_row)[:4]
        )
        delta_ref[12 + 4 * p : 16 + 4 * p, :] = (
            col_delta[heads]
            + col_far[heads]
            * head_sums(ga6[3 + p].astype(F32) * far_ref[p].astype(F32))[:4]
        )
    parts[0:12, :] = row_near
    parts[12:24, :] = row_far
    weights = jnp.transpose(parts[...])
    lane = lax.broadcasted_iota(jnp.int32, (N, N), 1)
    for p in range(3):
        for g in range(2):
            r = 4 * p + 2 * g
            near_weight = jnp.where(lane < HALF, weights[:, r : r + 1], weights[:, r + 1 : r + 2])
            far_weight = jnp.where(
                lane < HALF, weights[:, 12 + r : 13 + r], weights[:, 13 + r : 14 + r]
            )
            att_ref[p, :, N * g : N * g + N] = (
                near_weight * near_ref[p, :, N * g : N * g + N]
                + far_weight * stage[pl.ds(2 * p + g, N, stride=MIXED), :]
            ).astype(BF)
    dk6[3:] = jnp.zeros((3, N, 256), F32)
    dv6[3:] = jnp.zeros((3, N, 256), F32)

    def pair_step(b, c, g):
        lanes = slice(N * g, N * g + N)
        queries = stack(q6[b, :, lanes] * BF(FACTOR), masks)
        grads = stack(ga6[b, :, lanes], masks)
        r = 4 * b + 2 * g
        log_all = jnp.concatenate([log_all_ref[r : r + 1, :], log_all_ref[r + 1 : r + 2, :]], axis=1)
        delta = jnp.concatenate([delta_ref[r : r + 1, :], delta_ref[r + 1 : r + 2, :]], axis=1)
        keys = k6[c, :, lanes]
        prob = jnp.exp(nt(keys, queries) - log_all).astype(BF)
        step = (prob.astype(F32) * (nt(v6[c, :, lanes], grads) - delta)).astype(BF)
        tall = jnp.concatenate([step[:, :N], step[:, N:]], axis=0)
        return tn(tall, stack(keys, masks)) * FACTOR, nn(step, queries), nn(prob, grads)

    for b in range(3):
        for g in range(2):
            lanes = slice(N * g, N * g + N)
            dq_ref[b, :, lanes], dk6[b, :, lanes], dv6[b, :, lanes] = pair_step(b, b, g)
    for b in range(6):
        for g in range(2):
            lanes = slice(N * g, N * g + N)
            dq, dk, dv = pair_step(b, partner[b], g)
            if b < 3:
                dq_ref[b, :, lanes] += dq
            else:
                stage[pl.ds(2 * (b - 3) + g, N, stride=SENT), :] = dq
            dk6[partner[b], :, lanes] += dk
            dv6[partner[b], :, lanes] += dv
    for p in range(3):
        dk_ref[p] = dk6[p]
        dv_ref[p] = dv6[p]
        for g in range(2):
            lanes = slice(N * g, N * g + N)
            stage[pl.ds(6 + 2 * p + g, N, stride=SENT), :] = dk6[3 + p, :, lanes]
            stage[pl.ds(12 + 2 * p + g, N, stride=SENT), :] = dv6[3 + p, :, lanes]
    send_ref[...] = stage[...].astype(BF)


def finish_kernel(dq_ref, dk_ref, dv_ref, got_ref, q_out, k_out, v_out, stage):
    stage[...] = got_ref[...].astype(F32)
    for a, (mine, out) in enumerate(((dq_ref, q_out), (dk_ref, k_out), (dv_ref, v_out))):
        for p in range(3):
            for g in range(2):
                lanes = slice(N * g, N * g + N)
                rows = pl.ds(2 * (3 * a + p) + g, N, stride=SENT)
                out[p, :, lanes] = (mine[p, :, lanes] + stage[rows, :]).astype(BF)


def shape(*dims, dtype=BF):
    return jax.ShapeDtypeStruct(dims, dtype)


def cost(flops, moved):
    return pl.CostEstimate(flops=flops, bytes_accessed=moved, transcendentals=0)


def exchange(sent, rows):
    sent = sent.reshape(N, rows // 2, 2, N)
    got = lax.all_to_all(sent, "band", split_axis=0, concat_axis=0, tiled=True)
    return got.reshape(N * rows, N)


def body(queries, attn_keys, attn_values, out_proj, grad_out, plane_axes):
    me = lax.axis_index("head")
    swap = [(0, 1), (1, 0)]
    q, k, v = queries[0], attn_keys[0], attn_values[0]
    line = (3, N, 256)
    stage = pltpu.VMEM((SENT * N, N), F32)
    square = pltpu.VMEM((N, N), F32)

    own_cotangent = grad_out.reshape(3 * HALF, 1024)
    other_cotangent = lax.ppermute(own_cotangent, "head", swap)
    sent = pl.pallas_call(
        pack_lines_kernel,
        out_shape=shape(SENT * N, N),
        in_specs=[VMEM] * 3,
        out_specs=VMEM,
        scratch_shapes=[stage],
        compiler_params=PARAMS,
        name="pack_lines",
    )(q, k, v)
    lines = exchange(sent, SENT)
    grad_attended = pl.pallas_call(
        cotangent_kernel,
        out_shape=shape(*line),
        in_specs=[VMEM] * 3,
        out_specs=VMEM,
        compiler_params=PARAMS,
        cost_estimate=cost(2 * 384 * 1024 * 256, 1500000),
        name="cotangent",
    )(own_cotangent, other_cotangent, out_proj)

    sent, q6, k6, v6, near_out, far_out, totals = pl.pallas_call(
        forward_kernel,
        out_shape=(
            shape(MIXED * N, N),
            shape(6, N, 256),
            shape(6, N, 256),
            shape(6, N, 256),
            shape(*line, dtype=F32),
            shape(*line),
            shape(40, N, dtype=F32),
        ),
        in_specs=[SMEM] + [VMEM] * 5,
        out_specs=(VMEM,) * 7,
        scratch_shapes=[stage, square],
        compiler_params=PARAMS,
        name="forward",
    )(plane_axes, q, k, v, grad_attended, lines)
    mixed = exchange(sent, MIXED)

    attended, dq, dk, dv, sent = pl.pallas_call(
        backward_kernel,
        out_shape=(
            shape(*line),
            shape(*line, dtype=F32),
            shape(*line, dtype=F32),
            shape(*line, dtype=F32),
            shape(SENT * N, N),
        ),
        in_specs=[SMEM] + [VMEM] * 8,
        out_specs=(VMEM,) * 5,
        scratch_shapes=[
            stage,
            square,
            pltpu.VMEM((6, N, 256), BF),
            pltpu.VMEM((24, N), F32),
            pltpu.VMEM((24, N), F32),
            pltpu.VMEM((6, N, 256), F32),
            pltpu.VMEM((6, N, 256), F32),
        ],
        compiler_params=PARAMS,
        name="backward",
    )(plane_axes, q6, k6, v6, grad_attended, near_out, far_out, totals, mixed)
    returned = exchange(sent, SENT)

    def share(side):
        part = lax.dynamic_slice_in_dim(attended, side * HALF, HALF, axis=1)
        return jnp.dot(part.reshape(3 * HALF, 256), out_proj, preferred_element_type=F32)

    arrived = lax.ppermute(share(1 - me).astype(BF), "head", swap)
    layer_out = (share(me) + arrived.astype(F32)).astype(BF).reshape(1, 3, HALF, 1024)

    dq, dk, dv = pl.pallas_call(
        finish_kernel,
        out_shape=(shape(*line),) * 3,
        in_specs=[VMEM] * 4,
        out_specs=(VMEM,) * 3,
        scratch_shapes=[stage],
        compiler_params=PARAMS,
        name="finish",
    )(dq, dk, dv, returned)
    return layer_out, dq[None], dk[None], dv[None]


def solution(mesh):
    lines = P("band", None, None, "head")
    columns = P("band", None, "head", None)
    return jax.shard_map(
        body,
        mesh=mesh,
        in_specs=(lines, lines, lines, P("head", None), columns, P()),
        out_specs=(columns, lines, lines, lines),
        check_vma=False,
    )
```

```python
import jax
import jax.numpy as jnp
from jax import lax
from jax.experimental import pallas as pl
from jax.experimental.pallas import tpu as pltpu
from jax.sharding import PartitionSpec as P

BF = jnp.bfloat16
F32 = jnp.float32
N = 128
HALF = 64
SENT = 18
MIXED = 14
FACTOR = 0.125
LONG = 60 * 10**9
PARAMS = pltpu.CompilerParams(vmem_limit_bytes=48 * 1024 * 1024)
ROOMY = pltpu.CompilerParams(vmem_limit_bytes=60 * 1024 * 1024)
VMEM = pl.BlockSpec(memory_space=pltpu.VMEM)
SMEM = pl.BlockSpec(memory_space=pltpu.SMEM)


def nt(a, b):
    return lax.dot_general(a, b, (((1,), (1,)), ((), ())), preferred_element_type=F32)


def tn(a, b):
    return lax.dot_general(a, b, (((0,), (0,)), ((), ())), preferred_element_type=F32)


def nn(a, b):
    return lax.dot_general(a, b, (((1,), (0,)), ((), ())), preferred_element_type=F32)


def lane_masks():
    lane = lax.broadcasted_iota(jnp.int32, (N, N), 1)
    first = jnp.where(lane < HALF, 1.0, 0.0)
    return first.astype(BF), (1.0 - first).astype(BF)


def stack(x, masks):
    return jnp.concatenate([x * masks[0], x * masks[1]], axis=0)


def head_sums(product):
    row = lax.broadcasted_iota(jnp.int32, (8, 256), 0)
    lane = lax.broadcasted_iota(jnp.int32, (8, 256), 1)
    pick = jnp.where(lane // HALF == row, 1.0, 0.0).astype(BF)
    high = product.astype(BF)
    low = (product - high.astype(F32)).astype(BF)
    return nt(pick, high) + nt(pick, low)


def partners(axes_ref):
    axis = [axes_ref[b % 3, b // 3] for b in range(6)]
    found = []
    for b in range(6):
        other = jnp.int32(0)
        for c in range(6):
            if c != b:
                other = other + jnp.where(axis[c] == axis[b], jnp.int32(c), jnp.int32(0))
        found.append(other)
    return found


def pack_lines_kernel(q_ref, k_ref, v_ref, out_ref, held, stage, sems):
    copies = [
        pltpu.make_async_copy(ref, held.at[a], sems.at[a])
        for a, ref in enumerate((q_ref, k_ref, v_ref))
    ]
    for copy in copies:
        copy.start()
    for a, copy in enumerate(copies):
        copy.wait()
        for p in range(3):
            for g in range(2):
                rows = pl.ds(2 * (3 * a + p) + g, N, stride=SENT)
                stage[rows, :] = held[a, p, :, N * g : N * g + N].astype(F32)
    out_ref[...] = stage[...].astype(BF)


def cotangent_kernel(own_ref, other_ref, proj_ref, out_ref):
    me = lax.axis_index("head")
    for ref, side in ((own_ref, me), (other_ref, 1 - me)):
        made = nt(ref[...], proj_ref[...]).astype(BF)
        for p in range(3):
            out_ref[p, pl.ds(pl.multiple_of(side * HALF, HALF), HALF), :] = made[
                HALF * p : HALF * p + HALF
            ]


def forward_kernel(
    axes_ref, q_ref, k_ref, v_ref, ga_ref, got_ref,
    send_ref, q6, k6, v6, near_ref, far_ref, totals_ref,
    stage, parts,
):
    partner = partners(axes_ref)
    masks = lane_masks()
    stage[...] = got_ref[...].astype(F32)
    for a, (mine, six) in enumerate(((q_ref, q6), (k_ref, k6), (v_ref, v6))):
        for p in range(3):
            six[p] = mine[p]
            for g in range(2):
                rows = pl.ds(2 * (3 * a + p) + g, N, stride=SENT)
                six[3 + p, :, N * g : N * g + N] = stage[rows, :].astype(BF)
    for b in range(6):
        for g in range(2):
            lanes = slice(N * g, N * g + N)
            queries = stack(q6[b, :, lanes] * BF(FACTOR), masks)
            scores = [nt(k6[partner[b], :, lanes], queries)]
            values = [v6[partner[b], :, lanes]]
            if b < 3:
                scores.append(nt(k6[b, :, lanes], queries))
                values.append(v6[b, :, lanes])
            top = jnp.max(scores[0], axis=0, keepdims=True)
            for s in scores[1:]:
                top = jnp.maximum(top, jnp.max(s, axis=0, keepdims=True))
            raised = [jnp.exp(s - top) for s in scores]
            total = jnp.sum(raised[0], axis=0, keepdims=True)
            for e in raised[1:]:
                total = total + jnp.sum(e, axis=0, keepdims=True)
            scale = 1.0 / total
            total = top + jnp.log(total)
            out = None
            for e, v in zip(raised, values):
                prob = (e * scale).astype(BF)
                both = jnp.concatenate([prob[:, :N], prob[:, N:]], axis=0)
                term = tn(both, stack(v, masks))
                out = term if out is None else out + term
            row = (0 if b < 3 else 24) + 4 * (b % 3) + 2 * g
            totals_ref[row : row + 1, :] = total[:, :N]
            totals_ref[row + 1 : row + 2, :] = total[:, N:]
            if b < 3:
                near_ref[b, :, lanes] = out
            else:
                far_ref[b - 3, :, lanes] = out.astype(BF)
    for p in range(3):
        totals_ref[12 + 4 * p : 16 + 4 * p, :] = head_sums(
            ga_ref[p].astype(F32) * near_ref[p]
        )[:4]
    totals_ref[36:40, :] = jnp.zeros((4, N), F32)
    parts[...] = jnp.zeros((N, N), F32)
    left = totals_ref[...]
    for piece in range(3):
        rounded = left.astype(BF).astype(F32)
        parts[40 * piece : 40 * piece + 40, :] = rounded
        left = left - rounded
    stage[pl.ds(12, N, stride=MIXED), :] = jnp.transpose(parts[...])
    stage[pl.ds(13, N, stride=MIXED), :] = jnp.zeros((N, N), F32)
    for p in range(3):
        for g in range(2):
            lanes = slice(N * g, N * g + N)
            stage[pl.ds(2 * p + g, N, stride=MIXED), :] = far_ref[p, :, lanes].astype(F32)
            stage[pl.ds(6 + 2 * p + g, N, stride=MIXED), :] = ga_ref[p, :, lanes].astype(F32)
    send_ref[...] = stage[: MIXED * N, :].astype(BF)


def both_totals(near, far):
    top = jnp.maximum(near, far)
    log_all = top + jnp.log(jnp.exp(near - top) + jnp.exp(far - top))
    return log_all, jnp.exp(near - log_all), jnp.exp(far - log_all)


def merge_kernel(
    ga_ref, near_ref, far_ref, totals_ref, proj_ref, got_ref,
    ga_col_ref, log_all_ref, delta_ref, given_ref, kept_ref,
    stage, parts, att,
):
    stage[...] = got_ref[...].astype(F32)
    parts[...] = jnp.transpose(stage[pl.ds(12, N, stride=MIXED), :])
    arrived = parts[0:40, :] + (parts[40:80, :] + parts[80:120, :])
    for p in range(3):
        for g in range(2):
            ga_col_ref[p, :, N * g : N * g + N] = stage[
                pl.ds(6 + 2 * p + g, N, stride=MIXED), :
            ].astype(BF)
    row_log, row_near, row_far = both_totals(totals_ref[0:12, :], arrived[24:36])
    col_log, col_near, col_far = both_totals(arrived[0:12], totals_ref[24:36, :])
    log_all_ref[0:12, :] = row_log
    log_all_ref[12:24, :] = col_log
    row_delta = row_near * totals_ref[12:24, :]
    col_delta = col_near * arrived[12:24]
    for p in range(3):
        far_row = jnp.concatenate(
            [stage[pl.ds(2 * p + g, N, stride=MIXED), :] for g in range(2)], axis=1
        )
        heads = slice(4 * p, 4 * p + 4)
        delta_ref[4 * p : 4 * p + 4, :] = (
            row_delta[heads] + row_far[heads] * head_sums(ga_ref[p].astype(F32) * far_row)[:4]
        )
        delta_ref[12 + 4 * p : 16 + 4 * p, :] = (
            col_delta[heads]
            + col_far[heads]
            * head_sums(ga_col_ref[p].astype(F32) * far_ref[p].astype(F32))[:4]
        )
    parts[0:12, :] = row_near
    parts[12:24, :] = row_far
    weights = jnp.transpose(parts[...])
    lane = lax.broadcasted_iota(jnp.int32, (N, N), 1)
    for p in range(3):
        for g in range(2):
            r = 4 * p + 2 * g
            near_weight = jnp.where(lane < HALF, weights[:, r : r + 1], weights[:, r + 1 : r + 2])
            far_weight = jnp.where(
                lane < HALF, weights[:, 12 + r : 13 + r], weights[:, 13 + r : 14 + r]
            )
            att[p, :, N * g : N * g + N] = (
                near_weight * near_ref[p, :, N * g : N * g + N]
                + far_weight * stage[pl.ds(2 * p + g, N, stride=MIXED), :]
            ).astype(BF)
    me = lax.axis_index("head")
    for side, out in ((1 - me, given_ref), (me, kept_ref)):
        tokens = pl.ds(pl.multiple_of(side * HALF, HALF), HALF)
        for p in range(3):
            out[HALF * p : HALF * p + HALF, :] = nn(att[p, tokens, :], proj_ref[...]).astype(out.dtype)


def layer_kernel(kept_ref, got_ref, out_ref):
    out_ref[...] = (kept_ref[...] + got_ref[...].astype(F32)).astype(BF)


def backward_kernel(
    axes_ref, q6, k6, v6, ga_ref, ga_col_ref, log_all_ref, delta_ref,
    dq_ref, dk_ref, dv_ref, send_ref,
    stage, ga6, dk6, dv6,
):
    partner = partners(axes_ref)
    masks = lane_masks()
    for p in range(3):
        ga6[p] = ga_ref[p]
        ga6[3 + p] = ga_col_ref[p]
    dk6[3:] = jnp.zeros((3, N, 256), F32)
    dv6[3:] = jnp.zeros((3, N, 256), F32)

    def pair_step(b, c, g):
        lanes = slice(N * g, N * g + N)
        queries = stack(q6[b, :, lanes] * BF(FACTOR), masks)
        grads = stack(ga6[b, :, lanes], masks)
        r = 4 * b + 2 * g
        log_all = jnp.concatenate([log_all_ref[r : r + 1, :], log_all_ref[r + 1 : r + 2, :]], axis=1)
        delta = jnp.concatenate([delta_ref[r : r + 1, :], delta_ref[r + 1 : r + 2, :]], axis=1)
        keys = k6[c, :, lanes]
        prob = jnp.exp(nt(keys, queries) - log_all).astype(BF)
        step = (prob.astype(F32) * (nt(v6[c, :, lanes], grads) - delta)).astype(BF)
        tall = jnp.concatenate([step[:, :N], step[:, N:]], axis=0)
        return tn(tall, stack(keys, masks)) * FACTOR, nn(step, queries), nn(prob, grads)

    for b in range(3):
        for g in range(2):
            lanes = slice(N * g, N * g + N)
            dq_ref[b, :, lanes], dk6[b, :, lanes], dv6[b, :, lanes] = pair_step(b, b, g)
    for b in range(6):
        for g in range(2):
            lanes = slice(N * g, N * g + N)
            dq, dk, dv = pair_step(b, partner[b], g)
            if b < 3:
                dq_ref[b, :, lanes] += dq
            else:
                stage[pl.ds(2 * (b - 3) + g, N, stride=SENT), :] = dq
            dk6[partner[b], :, lanes] += dk
            dv6[partner[b], :, lanes] += dv
    for p in range(3):
        dk_ref[p] = dk6[p]
        dv_ref[p] = dv6[p]
        for g in range(2):
            lanes = slice(N * g, N * g + N)
            stage[pl.ds(6 + 2 * p + g, N, stride=SENT), :] = dk6[3 + p, :, lanes]
            stage[pl.ds(12 + 2 * p + g, N, stride=SENT), :] = dv6[3 + p, :, lanes]
    send_ref[...] = stage[...].astype(BF)


def finish_kernel(dq_ref, dk_ref, dv_ref, got_ref, q_out, k_out, v_out, stage):
    stage[...] = got_ref[...].astype(F32)
    for a, (mine, out) in enumerate(((dq_ref, q_out), (dk_ref, k_out), (dv_ref, v_out))):
        for p in range(3):
            for g in range(2):
                lanes = slice(N * g, N * g + N)
                rows = pl.ds(2 * (3 * a + p) + g, N, stride=SENT)
                out[p, :, lanes] = (mine[p, :, lanes] + stage[rows, :]).astype(BF)


def shape(*dims, dtype=BF):
    return jax.ShapeDtypeStruct(dims, dtype)


def cost(flops, moved):
    return pl.CostEstimate(flops=flops, bytes_accessed=moved, transcendentals=0)


def exchange(sent, rows):
    sent = sent.reshape(N, rows // 2, 2, N)
    got = lax.all_to_all(sent, "band", split_axis=0, concat_axis=0, tiled=True)
    return got.reshape(N * rows, N)


def body(queries, attn_keys, attn_values, out_proj, grad_out, plane_axes):
    swap = [(0, 1), (1, 0)]
    q, k, v = queries[0], attn_keys[0], attn_values[0]
    line = (3, N, 256)
    stage = pltpu.VMEM((SENT * N, N), F32)
    square = pltpu.VMEM((N, N), F32)

    own_cotangent = grad_out.reshape(3 * HALF, 1024)
    other_cotangent = lax.ppermute(own_cotangent, "head", swap)
    sent = pl.pallas_call(
        pack_lines_kernel,
        out_shape=shape(SENT * N, N),
        in_specs=[pl.BlockSpec(memory_space=pltpu.HBM)] * 3,
        out_specs=VMEM,
        scratch_shapes=[pltpu.VMEM((3, *line), BF), stage, pltpu.SemaphoreType.DMA((3,))],
        compiler_params=ROOMY,
        name="pack_lines",
    )(q, k, v)
    lines = exchange(sent, SENT)
    grad_attended = pl.pallas_call(
        cotangent_kernel,
        out_shape=shape(*line),
        in_specs=[VMEM] * 3,
        out_specs=VMEM,
        compiler_params=PARAMS,
        cost_estimate=cost(LONG, 1500000),
        name="cotangent",
    )(own_cotangent, other_cotangent, out_proj)

    sent, q6, k6, v6, near_out, far_out, totals = pl.pallas_call(
        forward_kernel,
        out_shape=(
            shape(MIXED * N, N),
            shape(6, N, 256),
            shape(6, N, 256),
            shape(6, N, 256),
            shape(*line, dtype=F32),
            shape(*line),
            shape(40, N, dtype=F32),
        ),
        in_specs=[SMEM] + [VMEM] * 5,
        out_specs=(VMEM,) * 7,
        scratch_shapes=[stage, square],
        compiler_params=PARAMS,
        name="forward",
    )(plane_axes, q, k, v, grad_attended, lines)
    mixed = exchange(sent, MIXED)

    tokens = (3 * HALF, 1024)
    ga_columns, log_all, delta, given, kept = pl.pallas_call(
        merge_kernel,
        out_shape=(
            shape(*line),
            shape(24, N, dtype=F32),
            shape(24, N, dtype=F32),
            shape(*tokens),
            shape(*tokens, dtype=F32),
        ),
        in_specs=[VMEM] * 6,
        out_specs=(VMEM,) * 5,
        scratch_shapes=[pltpu.VMEM((MIXED * N, N), F32), square, pltpu.VMEM(line, BF)],
        compiler_params=PARAMS,
        name="merge",
    )(grad_attended, near_out, far_out, totals, out_proj, mixed)
    arrived = lax.ppermute(given, "head", swap)
    dq, dk, dv, sent = pl.pallas_call(
        backward_kernel,
        out_shape=(
            shape(*line, dtype=F32),
            shape(*line, dtype=F32),
            shape(*line, dtype=F32),
            shape(SENT * N, N),
        ),
        in_specs=[SMEM] + [VMEM] * 7,
        out_specs=(VMEM,) * 4,
        scratch_shapes=[
            stage,
            pltpu.VMEM((6, N, 256), BF),
            pltpu.VMEM((6, N, 256), F32),
            pltpu.VMEM((6, N, 256), F32),
        ],
        compiler_params=PARAMS,
        name="backward",
    )(plane_axes, q6, k6, v6, grad_attended, ga_columns, log_all, delta)
    returned = exchange(sent, SENT)
    layer_out = pl.pallas_call(
        layer_kernel,
        out_shape=shape(*tokens),
        in_specs=[VMEM] * 2,
        out_specs=VMEM,
        compiler_params=PARAMS,
        cost_estimate=cost(LONG, 1500000),
        name="layer",
    )(kept, arrived).reshape(1, 3, HALF, 1024)

    dq, dk, dv = pl.pallas_call(
        finish_kernel,
        out_shape=(shape(*line),) * 3,
        in_specs=[VMEM] * 4,
        out_specs=(VMEM,) * 3,
        scratch_shapes=[stage],
        compiler_params=PARAMS,
        name="finish",
    )(dq, dk, dv, returned)
    return layer_out, dq[None], dk[None], dv[None]


def solution(mesh):
    lines = P("band", None, None, "head")
    columns = P("band", None, "head", None)
    return jax.shard_map(
        body,
        mesh=mesh,
        in_specs=(lines, lines, lines, P("head", None), columns, P()),
        out_specs=(columns, lines, lines, lines),
        check_vma=False,
    )
```

```python
import jax
import jax.numpy as jnp
from jax import lax
from jax.experimental import pallas as pl
from jax.experimental.pallas import tpu as pltpu
from jax.sharding import PartitionSpec as P

BF = jnp.bfloat16
F32 = jnp.float32
N = 128
HALF = 64
SENT = 18
MIXED = 14
UNROLL = True
FACTOR = 0.125
LONG = 60 * 10**9
PARAMS = pltpu.CompilerParams(vmem_limit_bytes=48 * 1024 * 1024)
ROOMY = pltpu.CompilerParams(vmem_limit_bytes=60 * 1024 * 1024)
VMEM = pl.BlockSpec(memory_space=pltpu.VMEM)
SMEM = pl.BlockSpec(memory_space=pltpu.SMEM)


def nt(a, b):
    return lax.dot_general(a, b, (((1,), (1,)), ((), ())), preferred_element_type=F32)


def tn(a, b):
    return lax.dot_general(a, b, (((0,), (0,)), ((), ())), preferred_element_type=F32)


def nn(a, b):
    return lax.dot_general(a, b, (((1,), (0,)), ((), ())), preferred_element_type=F32)


def lane_masks():
    lane = lax.broadcasted_iota(jnp.int32, (N, N), 1)
    first = jnp.where(lane < HALF, 1.0, 0.0)
    return first.astype(BF), (1.0 - first).astype(BF)


def stack(x, masks):
    return jnp.concatenate([x * masks[0], x * masks[1]], axis=0)


def head_sums(product):
    row = lax.broadcasted_iota(jnp.int32, (8, 256), 0)
    lane = lax.broadcasted_iota(jnp.int32, (8, 256), 1)
    pick = jnp.where(lane // HALF == row, 1.0, 0.0).astype(BF)
    high = product.astype(BF)
    low = (product - high.astype(F32)).astype(BF)
    return nt(pick, high) + nt(pick, low)


def partner_of(axes_ref, b):
    axis = axes_ref[lax.rem(b, 3), lax.div(b, 3)]
    found = jnp.int32(0)
    for c in range(6):
        same = jnp.logical_and(axes_ref[c % 3, c // 3] == axis, b != c)
        found = found + jnp.where(same, jnp.int32(c), jnp.int32(0))
    return found


def planes(step):
    lax.fori_loop(0, 3, lambda p, _: (step(p), 0)[1], 0, unroll=UNROLL)


def tall(x):
    return jnp.concatenate([x[:, :N], x[:, N:]], axis=0)


def wide(rows, r):
    return jnp.concatenate([rows[r : r + 1], rows[r + 1 : r + 2]], axis=1)


def spread(columns, r):
    lane = lax.broadcasted_iota(jnp.int32, (N, N), 1)
    return jnp.where(lane < HALF, columns[:, r : r + 1], columns[:, r + 1 : r + 2])


def pack_lines_kernel(q_ref, k_ref, v_ref, out_ref, held, stage, sems):
    copies = [
        pltpu.make_async_copy(ref, held.at[a], sems.at[a])
        for a, ref in enumerate((q_ref, k_ref, v_ref))
    ]
    for copy in copies:
        copy.start()
    for a, copy in enumerate(copies):
        copy.wait()
        for p in range(3):
            for g in range(2):
                rows = pl.ds(2 * (3 * a + p) + g, N, stride=SENT)
                stage[rows, :] = held[a, p, :, N * g : N * g + N].astype(F32)
    out_ref[...] = stage[...].astype(BF)


def own_kernel(
    own_ref, other_ref, proj_ref, q_ref, k_ref, v_ref,
    ga_ref, top_ref, sum_ref, out_ref,
):
    me = lax.axis_index("head")
    for ref, side in ((own_ref, me), (other_ref, 1 - me)):
        made = nt(ref[...], proj_ref[...]).astype(BF)
        for p in range(3):
            ga_ref[p, pl.ds(pl.multiple_of(side * HALF, HALF), HALF), :] = made[
                HALF * p : HALF * p + HALF
            ]
    masks = lane_masks()

    def step(p):
        for g in range(2):
            lanes = slice(N * g, N * g + N)
            scores = nt(k_ref[p, :, lanes], stack(q_ref[p, :, lanes] * BF(FACTOR), masks))
            top = jnp.max(scores, axis=0, keepdims=True)
            raised = jnp.exp(scores - top)
            top_ref[p, g] = top
            sum_ref[p, g] = jnp.sum(raised, axis=0, keepdims=True)
            out_ref[p, :, lanes] = tn(tall(raised.astype(BF)), stack(v_ref[p, :, lanes], masks))

    planes(step)


def forward_kernel(
    axes_ref, q_ref, k_ref, v_ref, ga_ref, top_ref, sum_ref, own_ref, got_ref,
    send_ref, q6, k6, v6, near_ref, far_ref, totals_ref,
    stage, parts, rows,
):
    masks = lane_masks()
    stage[...] = got_ref[...].astype(F32)
    for a, (mine, six) in enumerate(((q_ref, q6), (k_ref, k6), (v_ref, v6))):
        for p in range(3):
            six[p] = mine[p]
            for g in range(2):
                lines = pl.ds(2 * (3 * a + p) + g, N, stride=SENT)
                six[3 + p, :, N * g : N * g + N] = stage[lines, :].astype(BF)

    def step(p):
        for b in (p, p + 3):
            partner = partner_of(axes_ref, b)
            for g in range(2):
                lanes = slice(N * g, N * g + N)
                queries = stack(q6[b, :, lanes] * BF(FACTOR), masks)
                scores = nt(k6[partner, :, lanes], queries)
                top = jnp.max(scores, axis=0, keepdims=True)
                if b is p:
                    top = jnp.maximum(top, top_ref[p, g])
                    before = jnp.exp(top_ref[p, g] - top)
                raised = jnp.exp(scores - top)
                total = jnp.sum(raised, axis=0, keepdims=True)
                if b is p:
                    total = total + sum_ref[p, g] * before
                scale = 1.0 / total
                out = tn(tall((raised * scale).astype(BF)), stack(v6[partner, :, lanes], masks))
                total = top + jnp.log(total)
                if b is p:
                    rows[0, p, g] = total
                    rows[1, p, g] = before * scale
                    near_ref[p, :, lanes] = out
                else:
                    rows[2, p, g] = total
                    far_ref[p, :, lanes] = out.astype(BF)

    planes(step)
    totals_ref[...] = jnp.zeros((40, N), F32)
    parts[...] = jnp.zeros((N, N), F32)
    for p in range(3):
        for g in range(2):
            for h in range(2):
                r = 4 * p + 2 * g + h
                half = slice(N * h, N * h + N)
                totals_ref[r : r + 1, :] = rows[0, p, g, :, half]
                totals_ref[24 + r : 25 + r, :] = rows[2, p, g, :, half]
                parts[r : r + 1, :] = rows[1, p, g, :, half]
    weights = jnp.transpose(parts[...])
    for p in range(3):
        for g in range(2):
            lanes = slice(N * g, N * g + N)
            near_ref[p, :, lanes] += spread(weights, 4 * p + 2 * g) * own_ref[p, :, lanes]
        totals_ref[12 + 4 * p : 16 + 4 * p, :] = head_sums(
            ga_ref[p].astype(F32) * near_ref[p]
        )[:4]
    left = totals_ref[...]
    for piece in range(3):
        rounded = left.astype(BF).astype(F32)
        parts[40 * piece : 40 * piece + 40, :] = rounded
        left = left - rounded
    stage[pl.ds(12, N, stride=MIXED), :] = jnp.transpose(parts[...])
    stage[pl.ds(13, N, stride=MIXED), :] = jnp.zeros((N, N), F32)
    for p in range(3):
        for g in range(2):
            lanes = slice(N * g, N * g + N)
            stage[pl.ds(2 * p + g, N, stride=MIXED), :] = far_ref[p, :, lanes].astype(F32)
            stage[pl.ds(6 + 2 * p + g, N, stride=MIXED), :] = ga_ref[p, :, lanes].astype(F32)
    send_ref[...] = stage[: MIXED * N, :].astype(BF)


def ready_kernel(axes_ref, q6, k6, v6, ga_ref, totals_ref, own_ref, near_ref, far_ref, own_dot, near_dot, rows):
    masks = lane_masks()
    for p in range(3):
        for g in range(2):
            r = 4 * p + 2 * g
            rows[0, p, g] = wide(totals_ref[0:12, :], r)
            rows[1, p, g] = wide(totals_ref[24:36, :], r)

    def step(p):
        near, far = partner_of(axes_ref, p), partner_of(axes_ref, p + 3)
        for g in range(2):
            lanes = slice(N * g, N * g + N)
            queries = stack(q6[p, :, lanes] * BF(FACTOR), masks)
            grads = stack(ga_ref[p, :, lanes], masks)
            total = rows[0, p, g]
            own_ref[p, g] = jnp.exp(nt(k6[p, :, lanes], queries) - total).astype(BF)
            near_ref[p, g] = jnp.exp(nt(k6[near, :, lanes], queries) - total).astype(BF)
            own_dot[p, g] = nt(v6[p, :, lanes], grads)
            near_dot[p, g] = nt(v6[near, :, lanes], grads)
            queries = stack(q6[p + 3, :, lanes] * BF(FACTOR), masks)
            far_ref[p, g] = jnp.exp(nt(k6[far, :, lanes], queries) - rows[1, p, g]).astype(BF)

    planes(step)


def both_weights(near, far):
    top = jnp.maximum(near, far)
    log_all = top + jnp.log(jnp.exp(near - top) + jnp.exp(far - top))
    return jnp.exp(near - log_all), jnp.exp(far - log_all)


def merge_kernel(
    ga_ref, near_ref, far_ref, totals_ref, proj_ref, got_ref, first_ref,
    ga_col_ref, weight_ref, delta_ref, given_ref, kept_ref,
    stage, parts, att,
):
    stage[...] = got_ref[...].astype(F32)
    parts[...] = jnp.transpose(stage[pl.ds(12, N, stride=MIXED), :])
    arrived = parts[0:40, :] + (parts[40:80, :] + parts[80:120, :])
    for p in range(3):
        for g in range(2):
            ga_col_ref[p, :, N * g : N * g + N] = stage[
                pl.ds(6 + 2 * p + g, N, stride=MIXED), :
            ].astype(BF)
    row_near, row_far = both_weights(totals_ref[0:12, :], arrived[24:36])
    col_near, col_far = both_weights(arrived[0:12], totals_ref[24:36, :])
    row_delta = row_near * totals_ref[12:24, :]
    col_delta = col_near * arrived[12:24]
    for p in range(3):
        far_row = jnp.concatenate(
            [stage[pl.ds(2 * p + g, N, stride=MIXED), :] for g in range(2)], axis=1
        )
        heads = slice(4 * p, 4 * p + 4)
        row_sums = head_sums(ga_ref[p].astype(F32) * far_row)[:4]
        col_sums = head_sums(ga_col_ref[p].astype(F32) * far_ref[p].astype(F32))[:4]
        row = row_delta[heads] + row_far[heads] * row_sums
        col = col_delta[heads] + col_far[heads] * col_sums
        for g in range(2):
            weight_ref[p, g] = wide(row_near, 4 * p + 2 * g)
            weight_ref[3 + p, g] = wide(col_far, 4 * p + 2 * g)
            delta_ref[p, g] = wide(row, 2 * g)
            delta_ref[3 + p, g] = wide(col, 2 * g)
    parts[0:12, :] = row_near
    parts[12:24, :] = row_far
    weights = jnp.transpose(parts[...])
    for p in range(3):
        for g in range(2):
            r = 4 * p + 2 * g
            att[p, :, N * g : N * g + N] = (
                spread(weights, r) * near_ref[p, :, N * g : N * g + N]
                + spread(weights, 12 + r) * stage[pl.ds(2 * p + g, N, stride=MIXED), :]
            ).astype(BF)
    me = lax.axis_index("head")
    for side, out in ((1 - me, given_ref), (me, kept_ref)):
        tokens = pl.ds(pl.multiple_of(side * HALF, HALF), HALF)
        for p in range(3):
            out[HALF * p : HALF * p + HALF, :] = nn(att[p, tokens, :], proj_ref[...]).astype(out.dtype)


def layer_kernel(kept_ref, got_ref, out_ref):
    out_ref[...] = (kept_ref[...] + got_ref[...].astype(F32)).astype(BF)


def backward_kernel(
    axes_ref, q6, k6, v6, ga_ref, ga_col_ref, own_p, near_p, far_p, own_dot, near_dot, weight_ref, delta_ref,
    dq_ref, dk_ref, dv_ref, send_ref,
    stage, dq_col, dk6, dv6,
):
    masks = lane_masks()

    def pair_step(b, c, g, prob, dots, queries, grads):
        lanes = slice(N * g, N * g + N)
        prob = prob.astype(F32) * weight_ref[b, g]
        step = (prob * (dots - delta_ref[b, g])).astype(BF)
        dq = tn(tall(step), stack(k6[c, :, lanes], masks))
        return dq, nn(step, queries), nn(prob.astype(BF), grads)

    def first(p):
        for g in range(2):
            lanes = slice(N * g, N * g + N)
            queries = stack(q6[p, :, lanes] * BF(FACTOR), masks)
            grads = stack(ga_ref[p, :, lanes], masks)
            dq_ref[p, :, lanes], dk6[p, :, lanes], dv6[p, :, lanes] = pair_step(
                p, p, g, own_p[p, g], own_dot[p, g], queries, grads
            )
            dk6[p + 3, :, lanes] = jnp.zeros((N, N), F32)
            dv6[p + 3, :, lanes] = jnp.zeros((N, N), F32)

    def second(p):
        near, far = partner_of(axes_ref, p), partner_of(axes_ref, p + 3)
        for g in range(2):
            lanes = slice(N * g, N * g + N)
            queries = stack(q6[p, :, lanes] * BF(FACTOR), masks)
            grads = stack(ga_ref[p, :, lanes], masks)
            dq, dk, dv = pair_step(p, near, g, near_p[p, g], near_dot[p, g], queries, grads)
            dq_ref[p, :, lanes] = (dq_ref[p, :, lanes] + dq) * FACTOR
            dk6[near, :, lanes] += dk
            dv6[near, :, lanes] += dv
            queries = stack(q6[p + 3, :, lanes] * BF(FACTOR), masks)
            grads = stack(ga_col_ref[p, :, lanes], masks)
            dots = nt(v6[far, :, lanes], grads)
            dq, dk, dv = pair_step(p + 3, far, g, far_p[p, g], dots, queries, grads)
            dq_col[p, :, lanes] = dq * FACTOR
            dk6[far, :, lanes] += dk
            dv6[far, :, lanes] += dv

    planes(first)
    planes(second)
    for p in range(3):
        dk_ref[p] = dk6[p]
        dv_ref[p] = dv6[p]
        for g in range(2):
            lanes = slice(N * g, N * g + N)
            stage[pl.ds(2 * p + g, N, stride=SENT), :] = dq_col[p, :, lanes]
            stage[pl.ds(6 + 2 * p + g, N, stride=SENT), :] = dk6[3 + p, :, lanes]
            stage[pl.ds(12 + 2 * p + g, N, stride=SENT), :] = dv6[3 + p, :, lanes]
    send_ref[...] = stage[...].astype(BF)


def finish_kernel(dq_ref, dk_ref, dv_ref, got_ref, q_out, k_out, v_out, stage):
    stage[...] = got_ref[...].astype(F32)
    for a, (mine, out) in enumerate(((dq_ref, q_out), (dk_ref, k_out), (dv_ref, v_out))):
        for p in range(3):
            for g in range(2):
                lanes = slice(N * g, N * g + N)
                rows = pl.ds(2 * (3 * a + p) + g, N, stride=SENT)
                out[p, :, lanes] = (mine[p, :, lanes] + stage[rows, :]).astype(BF)


def shape(*dims, dtype=BF):
    return jax.ShapeDtypeStruct(dims, dtype)


def cost(flops, moved):
    return pl.CostEstimate(flops=flops, bytes_accessed=moved, transcendentals=0)


def exchange(sent, rows):
    sent = sent.reshape(N, rows // 2, 2, N)
    got = lax.all_to_all(sent, "band", split_axis=0, concat_axis=0, tiled=True)
    return got.reshape(N * rows, N)


LINE = (3, N, 256)
TOKENS = (3 * HALF, 1024)
PAIR = (3, 2, N, 256)
ROW = (3, 2, 1, 256)
STAGE = pltpu.VMEM((SENT * N, N), F32)
SQUARE = pltpu.VMEM((N, N), F32)


def call(kernel, ins, outs, scratch, name, params=PARAMS, estimate=None):
    many = len(outs) > 1
    return pl.pallas_call(
        kernel,
        out_shape=tuple(outs) if many else outs[0],
        in_specs=[SMEM if x.dtype == jnp.int32 else VMEM for x in ins],
        out_specs=(VMEM,) * len(outs) if many else VMEM,
        scratch_shapes=scratch,
        compiler_params=params,
        cost_estimate=estimate,
        name=name,
    )(*ins)


def own(*ins):
    outs = [shape(*LINE), shape(*ROW, dtype=F32), shape(*ROW, dtype=F32), shape(*LINE, dtype=F32)]
    return call(own_kernel, ins, outs, [], "own", estimate=cost(LONG, 3000000))


def forward(*ins):
    outs = [shape(MIXED * N, N)] + [shape(6, N, 256)] * 3
    outs += [shape(*LINE, dtype=F32), shape(*LINE), shape(40, N, dtype=F32)]
    return call(forward_kernel, ins, outs, [STAGE, SQUARE, pltpu.VMEM((3, *ROW), F32)], "forward")


def ready(*ins):
    outs = [shape(*PAIR)] * 3 + [shape(*PAIR, dtype=F32)] * 2
    return call(ready_kernel, ins, outs, [pltpu.VMEM((2, *ROW), F32)], "ready", estimate=cost(10**9, 3000000))


def merge(*ins):
    rows = shape(6, 2, 1, 256, dtype=F32)
    outs = [shape(*LINE), rows, rows, shape(*TOKENS), shape(*TOKENS, dtype=F32)]
    scratch = [pltpu.VMEM((MIXED * N, N), F32), SQUARE, pltpu.VMEM(LINE, BF)]
    return call(merge_kernel, ins, outs, scratch, "merge")


def backward(*ins):
    outs = [shape(*LINE, dtype=F32)] * 3 + [shape(SENT * N, N)]
    scratch = [STAGE, pltpu.VMEM(LINE, F32)] + [pltpu.VMEM((6, N, 256), F32)] * 2
    return call(backward_kernel, ins, outs, scratch, "backward")


def finish(*ins):
    return call(finish_kernel, ins, [shape(*LINE)] * 3, [STAGE], "finish")


def pack_lines(*ins):
    return pl.pallas_call(
        pack_lines_kernel,
        out_shape=shape(SENT * N, N),
        in_specs=[pl.BlockSpec(memory_space=pltpu.HBM)] * 3,
        out_specs=VMEM,
        scratch_shapes=[pltpu.VMEM((3, *LINE), BF), STAGE, pltpu.SemaphoreType.DMA((3,))],
        compiler_params=ROOMY,
        name="pack_lines",
    )(*ins)


def body(queries, attn_keys, attn_values, out_proj, grad_out, plane_axes):
    swap = [(0, 1), (1, 0)]
    q, k, v = queries[0], attn_keys[0], attn_values[0]

    cotangent = grad_out.reshape(TOKENS)
    other = lax.ppermute(cotangent, "head", swap)
    lines = exchange(pack_lines(q, k, v), SENT)
    ga, top, total, own_out = own(cotangent, other, out_proj, q, k, v)

    sent, q6, k6, v6, near_out, far_out, totals = forward(
        plane_axes, q, k, v, ga, top, total, own_out, lines
    )
    mixed = exchange(sent, MIXED)
    own_p, near_p, far_p, own_dot, near_dot = ready(plane_axes, q6, k6, v6, ga, totals)

    ga_columns, weight, delta, given, kept = merge(
        ga, near_out, far_out, totals, out_proj, mixed, own_p
    )
    arrived = lax.ppermute(given, "head", swap)
    dq, dk, dv, sent = backward(
        plane_axes, q6, k6, v6, ga, ga_columns, own_p, near_p, far_p, own_dot, near_dot, weight, delta
    )
    returned = exchange(sent, SENT)
    layer = call(
        layer_kernel, (kept, arrived), [shape(*TOKENS)], [], "layer", estimate=cost(LONG, 1500000)
    )
    dq, dk, dv = finish(dq, dk, dv, returned)
    return layer.reshape(1, 3, HALF, 1024), dq[None], dk[None], dv[None]


def solution(mesh):
    lines = P("band", None, None, "head")
    columns = P("band", None, "head", None)
    return jax.shard_map(
        body,
        mesh=mesh,
        in_specs=(lines, lines, lines, P("head", None), columns, P()),
        out_specs=(columns, lines, lines, lines),
        check_vma=False,
    )
```

```python
import jax
import jax.numpy as jnp
from jax import lax
from jax.experimental import pallas as pl
from jax.experimental.pallas import tpu as pltpu
from jax.sharding import PartitionSpec as P

BF = jnp.bfloat16
F32 = jnp.float32
N = 128
HALF = 64
SENT = 18
MIXED = 14
UNROLL = True
FACTOR = 0.125
LONG = 60 * 10**9
PARAMS = pltpu.CompilerParams(vmem_limit_bytes=48 * 1024 * 1024)
ROOMY = pltpu.CompilerParams(vmem_limit_bytes=60 * 1024 * 1024)
VMEM = pl.BlockSpec(memory_space=pltpu.VMEM)
SMEM = pl.BlockSpec(memory_space=pltpu.SMEM)


def nt(a, b):
    return lax.dot_general(a, b, (((1,), (1,)), ((), ())), preferred_element_type=F32)


def tn(a, b):
    return lax.dot_general(a, b, (((0,), (0,)), ((), ())), preferred_element_type=F32)


def nn(a, b):
    return lax.dot_general(a, b, (((1,), (0,)), ((), ())), preferred_element_type=F32)


def lane_masks():
    lane = lax.broadcasted_iota(jnp.int32, (N, N), 1)
    first = jnp.where(lane < HALF, 1.0, 0.0)
    return first.astype(BF), (1.0 - first).astype(BF)


def stack(x, masks):
    return jnp.concatenate([x * masks[0], x * masks[1]], axis=0)


def head_sums(product):
    row = lax.broadcasted_iota(jnp.int32, (8, 256), 0)
    lane = lax.broadcasted_iota(jnp.int32, (8, 256), 1)
    pick = jnp.where(lane // HALF == row, 1.0, 0.0).astype(BF)
    high = product.astype(BF)
    low = (product - high.astype(F32)).astype(BF)
    return nt(pick, high) + nt(pick, low)


def partner_of(axes_ref, b):
    axis = axes_ref[lax.rem(b, 3), lax.div(b, 3)]
    found = jnp.int32(0)
    for c in range(6):
        same = jnp.logical_and(axes_ref[c % 3, c // 3] == axis, b != c)
        found = found + jnp.where(same, jnp.int32(c), jnp.int32(0))
    return found


def planes(step):
    lax.fori_loop(0, 3, lambda p, _: (step(p), 0)[1], 0, unroll=UNROLL)


def tall(x):
    return jnp.concatenate([x[:, :N], x[:, N:]], axis=0)


def wide(rows, r):
    return jnp.concatenate([rows[r : r + 1], rows[r + 1 : r + 2]], axis=1)


def spread(columns, r):
    lane = lax.broadcasted_iota(jnp.int32, (N, N), 1)
    return jnp.where(lane < HALF, columns[:, r : r + 1], columns[:, r + 1 : r + 2])


def pack_lines_kernel(q_ref, k_ref, v_ref, out_ref, held, stage, sems):
    copies = [
        pltpu.make_async_copy(ref, held.at[a], sems.at[a])
        for a, ref in enumerate((q_ref, k_ref, v_ref))
    ]
    for copy in copies:
        copy.start()
    for a, copy in enumerate(copies):
        copy.wait()
        for p in range(3):
            for g in range(2):
                rows = pl.ds(2 * (3 * a + p) + g, N, stride=SENT)
                stage[rows, :] = held[a, p, :, N * g : N * g + N].astype(F32)
    out_ref[...] = stage[...].astype(BF)


def own_kernel(
    own_ref, other_ref, proj_ref, q_ref, k_ref, v_ref,
    ga_ref, top_ref, sum_ref, out_ref,
):
    me = lax.axis_index("head")
    for ref, side in ((own_ref, me), (other_ref, 1 - me)):
        made = nt(ref[...], proj_ref[...]).astype(BF)
        for p in range(3):
            ga_ref[p, pl.ds(pl.multiple_of(side * HALF, HALF), HALF), :] = made[
                HALF * p : HALF * p + HALF
            ]
    masks = lane_masks()

    def step(p):
        for g in range(2):
            lanes = slice(N * g, N * g + N)
            scores = nt(k_ref[p, :, lanes], stack(q_ref[p, :, lanes] * BF(FACTOR), masks))
            top = jnp.max(scores, axis=0, keepdims=True)
            raised = jnp.exp(scores - top)
            top_ref[p, g] = top
            sum_ref[p, g] = jnp.sum(raised, axis=0, keepdims=True)
            out_ref[p, :, lanes] = tn(tall(raised.astype(BF)), stack(v_ref[p, :, lanes], masks))

    planes(step)


def forward_kernel(
    axes_ref, q_ref, k_ref, v_ref, ga_ref, top_ref, sum_ref, own_ref, got_ref,
    send_ref, q6, k6, v6, near_ref, far_ref, totals_ref,
    stage, parts, rows, probs,
):
    masks = lane_masks()
    stage[...] = got_ref[...].astype(F32)
    for a, (mine, six) in enumerate(((q_ref, q6), (k_ref, k6), (v_ref, v6))):
        for p in range(3):
            six[p] = mine[p]
            for g in range(2):
                lines = pl.ds(2 * (3 * a + p) + g, N, stride=SENT)
                six[3 + p, :, N * g : N * g + N] = stage[lines, :].astype(BF)

    blocks = [(b, partner_of(axes_ref, b)) for b in range(6)]
    for g in range(2):
        lanes = slice(N * g, N * g + N)
        for b, c in blocks:
            p = b % 3
            scores = nt(k6[c, :, lanes], stack(q6[b, :, lanes] * BF(FACTOR), masks))
            top = jnp.max(scores, axis=0, keepdims=True)
            if b < 3:
                top = jnp.maximum(top, top_ref[p, g])
                before = jnp.exp(top_ref[p, g] - top)
            raised = jnp.exp(scores - top)
            total = jnp.sum(raised, axis=0, keepdims=True)
            if b < 3:
                total = total + sum_ref[p, g] * before
            scale = 1.0 / total
            probs[2 * b + g] = (raised * scale).astype(BF)
            rows[b // 3, p, g] = top + jnp.log(total)
            if b < 3:
                rows[2, p, g] = before * scale
    for g in range(2):
        lanes = slice(N * g, N * g + N)
        for b, c in blocks:
            out = tn(tall(probs[2 * b + g]), stack(v6[c, :, lanes], masks))
            if b < 3:
                near_ref[b, :, lanes] = out
            else:
                far_ref[b - 3, :, lanes] = out.astype(BF)
    totals_ref[...] = jnp.zeros((40, N), F32)
    parts[...] = jnp.zeros((N, N), F32)
    for p in range(3):
        for g in range(2):
            for h in range(2):
                r = 4 * p + 2 * g + h
                half = slice(N * h, N * h + N)
                totals_ref[r : r + 1, :] = rows[0, p, g, :, half]
                totals_ref[24 + r : 25 + r, :] = rows[1, p, g, :, half]
                parts[r : r + 1, :] = rows[2, p, g, :, half]
    weights = jnp.transpose(parts[...])
    for p in range(3):
        for g in range(2):
            lanes = slice(N * g, N * g + N)
            near_ref[p, :, lanes] += spread(weights, 4 * p + 2 * g) * own_ref[p, :, lanes]
        totals_ref[12 + 4 * p : 16 + 4 * p, :] = head_sums(
            ga_ref[p].astype(F32) * near_ref[p]
        )[:4]
    left = totals_ref[...]
    for piece in range(3):
        rounded = left.astype(BF).astype(F32)
        parts[40 * piece : 40 * piece + 40, :] = rounded
        left = left - rounded
    stage[pl.ds(12, N, stride=MIXED), :] = jnp.transpose(parts[...])
    stage[pl.ds(13, N, stride=MIXED), :] = jnp.zeros((N, N), F32)
    for p in range(3):
        for g in range(2):
            lanes = slice(N * g, N * g + N)
            stage[pl.ds(2 * p + g, N, stride=MIXED), :] = far_ref[p, :, lanes].astype(F32)
            stage[pl.ds(6 + 2 * p + g, N, stride=MIXED), :] = ga_ref[p, :, lanes].astype(F32)
    send_ref[...] = stage[: MIXED * N, :].astype(BF)


def both_weights(near, far):
    top = jnp.maximum(near, far)
    log_all = top + jnp.log(jnp.exp(near - top) + jnp.exp(far - top))
    return log_all, jnp.exp(near - log_all), jnp.exp(far - log_all)


def merge_kernel(
    ga_ref, near_ref, far_ref, totals_ref, proj_ref, got_ref,
    ga_col_ref, log_all_ref, delta_ref, given_ref, kept_ref,
    stage, parts, att,
):
    stage[...] = got_ref[...].astype(F32)
    parts[...] = jnp.transpose(stage[pl.ds(12, N, stride=MIXED), :])
    arrived = parts[0:40, :] + (parts[40:80, :] + parts[80:120, :])
    for p in range(3):
        for g in range(2):
            ga_col_ref[p, :, N * g : N * g + N] = stage[
                pl.ds(6 + 2 * p + g, N, stride=MIXED), :
            ].astype(BF)
    row_log, row_near, row_far = both_weights(totals_ref[0:12, :], arrived[24:36])
    col_log, col_near, col_far = both_weights(arrived[0:12], totals_ref[24:36, :])
    row_delta = row_near * totals_ref[12:24, :]
    col_delta = col_near * arrived[12:24]
    for p in range(3):
        far_row = jnp.concatenate(
            [stage[pl.ds(2 * p + g, N, stride=MIXED), :] for g in range(2)], axis=1
        )
        heads = slice(4 * p, 4 * p + 4)
        row_sums = head_sums(ga_ref[p].astype(F32) * far_row)[:4]
        col_sums = head_sums(ga_col_ref[p].astype(F32) * far_ref[p].astype(F32))[:4]
        row = row_delta[heads] + row_far[heads] * row_sums
        col = col_delta[heads] + col_far[heads] * col_sums
        for g in range(2):
            log_all_ref[p, g] = wide(row_log, 4 * p + 2 * g)
            log_all_ref[3 + p, g] = wide(col_log, 4 * p + 2 * g)
            delta_ref[p, g] = wide(row, 2 * g)
            delta_ref[3 + p, g] = wide(col, 2 * g)
    parts[0:12, :] = row_near
    parts[12:24, :] = row_far
    weights = jnp.transpose(parts[...])
    for p in range(3):
        for g in range(2):
            r = 4 * p + 2 * g
            att[p, :, N * g : N * g + N] = (
                spread(weights, r) * near_ref[p, :, N * g : N * g + N]
                + spread(weights, 12 + r) * stage[pl.ds(2 * p + g, N, stride=MIXED), :]
            ).astype(BF)
    me = lax.axis_index("head")
    for side, out in ((1 - me, given_ref), (me, kept_ref)):
        tokens = pl.ds(pl.multiple_of(side * HALF, HALF), HALF)
        for p in range(3):
            out[HALF * p : HALF * p + HALF, :] = nn(att[p, tokens, :], proj_ref[...]).astype(out.dtype)


def layer_kernel(kept_ref, got_ref, out_ref):
    out_ref[...] = (kept_ref[...] + got_ref[...].astype(F32)).astype(BF)


def backward_kernel(
    axes_ref, q6, k6, v6, ga_ref, ga_col_ref, log_all_ref, delta_ref,
    dq_ref, dk_ref, dv_ref, send_ref,
    stage, ga6, dq6, probs, steps,
):
    masks = lane_masks()

    def pair_step(b, c, g, queries, grads):
        lanes = slice(N * g, N * g + N)
        keys = k6[c, :, lanes]
        prob = jnp.exp(nt(keys, queries) - log_all_ref[b, g]).astype(BF)
        step = (prob.astype(F32) * (nt(v6[c, :, lanes], grads) - delta_ref[b, g])).astype(BF)
        return tn(tall(step), stack(keys, masks)), nn(step, queries), nn(prob, grads)

    def operands(b, g):
        lanes = slice(N * g, N * g + N)
        return stack(q6[b, :, lanes] * BF(FACTOR), masks), stack(ga6[b, :, lanes], masks)

    for p in range(3):
        ga6[p] = ga_ref[p]
        ga6[p + 3] = ga_col_ref[p]

    units = [(c, c) for c in range(3)] + [(partner_of(axes_ref, c), c) for c in range(6)]
    for g in range(2):
        lanes = slice(N * g, N * g + N)
        for u, (b, c) in enumerate(units):
            queries = stack(q6[b, :, lanes] * BF(FACTOR), masks)
            prob = jnp.exp(nt(k6[c, :, lanes], queries) - log_all_ref[b, g]).astype(BF)
            probs[2 * u + g] = prob
            steps[2 * u + g] = (prob.astype(F32) * (nt(v6[c, :, lanes], stack(ga6[b, :, lanes], masks)) - delta_ref[b, g])).astype(BF)
    for g in range(2):
        lanes = slice(N * g, N * g + N)
        for u, (b, c) in enumerate(units):
            queries, grads = operands(b, g)
            step = steps[2 * u + g]
            dq = tn(tall(step), stack(k6[c, :, lanes], masks))
            dk = nn(step, queries)
            dv = nn(probs[2 * u + g], grads)
            if u < 3:
                dq_ref[c, :, lanes] = dq
                dk_ref[c, :, lanes] = dk
                dv_ref[c, :, lanes] = dv
            else:
                dq6[b, :, lanes] = dq
                if c < 3:
                    dk_ref[c, :, lanes] += dk
                    dv_ref[c, :, lanes] += dv
                else:
                    stage[pl.ds(2 * c + g, N, stride=SENT), :] = dk
                    stage[pl.ds(6 + 2 * c + g, N, stride=SENT), :] = dv
    for p in range(3):
        dq_ref[p] = (dq_ref[p] + dq6[p]) * FACTOR
        for g in range(2):
            lanes = slice(N * g, N * g + N)
            stage[pl.ds(2 * p + g, N, stride=SENT), :] = dq6[3 + p, :, lanes] * FACTOR
    send_ref[...] = stage[...].astype(BF)


def finish_kernel(dq_ref, dk_ref, dv_ref, got_ref, q_out, k_out, v_out, stage):
    stage[...] = got_ref[...].astype(F32)
    for a, (mine, out) in enumerate(((dq_ref, q_out), (dk_ref, k_out), (dv_ref, v_out))):
        for p in range(3):
            for g in range(2):
                lanes = slice(N * g, N * g + N)
                rows = pl.ds(2 * (3 * a + p) + g, N, stride=SENT)
                out[p, :, lanes] = (mine[p, :, lanes] + stage[rows, :]).astype(BF)


def shape(*dims, dtype=BF):
    return jax.ShapeDtypeStruct(dims, dtype)


def cost(flops, moved):
    return pl.CostEstimate(flops=flops, bytes_accessed=moved, transcendentals=0)


def exchange(sent, rows):
    sent = sent.reshape(N, rows // 2, 2, N)
    got = lax.all_to_all(sent, "band", split_axis=0, concat_axis=0, tiled=True)
    return got.reshape(N * rows, N)


LINE = (3, N, 256)
TOKENS = (3 * HALF, 1024)
PAIR = (3, 2, N, 256)
ROW = (3, 2, 1, 256)
STAGE = pltpu.VMEM((SENT * N, N), F32)
SQUARE = pltpu.VMEM((N, N), F32)


def call(kernel, ins, outs, scratch, name, params=PARAMS, estimate=None):
    many = len(outs) > 1
    return pl.pallas_call(
        kernel,
        out_shape=tuple(outs) if many else outs[0],
        in_specs=[SMEM if x.dtype == jnp.int32 else VMEM for x in ins],
        out_specs=(VMEM,) * len(outs) if many else VMEM,
        scratch_shapes=scratch,
        compiler_params=params,
        cost_estimate=estimate,
        name=name,
    )(*ins)


def own(*ins):
    outs = [shape(*LINE), shape(*ROW, dtype=F32), shape(*ROW, dtype=F32), shape(*LINE, dtype=F32)]
    return call(own_kernel, ins, outs, [], "own", estimate=cost(LONG, 3000000))


def forward(*ins):
    outs = [shape(MIXED * N, N)] + [shape(6, N, 256)] * 3
    outs += [shape(*LINE, dtype=F32), shape(*LINE), shape(40, N, dtype=F32)]
    return call(forward_kernel, ins, outs, [STAGE, SQUARE, pltpu.VMEM((3, *ROW), F32), pltpu.VMEM((12, N, 256), BF)], "forward")


def merge(*ins):
    rows = shape(6, 2, 1, 256, dtype=F32)
    outs = [shape(*LINE), rows, rows, shape(*TOKENS), shape(*TOKENS, dtype=F32)]
    scratch = [pltpu.VMEM((MIXED * N, N), F32), SQUARE, pltpu.VMEM(LINE, BF)]
    return call(merge_kernel, ins, outs, scratch, "merge")


def backward(*ins):
    outs = [shape(*LINE, dtype=F32)] * 3 + [shape(SENT * N, N)]
    scratch = [STAGE, pltpu.VMEM((6, N, 256), BF), pltpu.VMEM((6, N, 256), F32)]
    scratch += [pltpu.VMEM((18, N, 256), BF), pltpu.VMEM((18, N, 256), BF)]
    return call(backward_kernel, ins, outs, scratch, "backward")


def finish(*ins):
    return call(finish_kernel, ins, [shape(*LINE)] * 3, [STAGE], "finish")


def pack_lines(*ins):
    return pl.pallas_call(
        pack_lines_kernel,
        out_shape=shape(SENT * N, N),
        in_specs=[pl.BlockSpec(memory_space=pltpu.HBM)] * 3,
        out_specs=VMEM,
        scratch_shapes=[pltpu.VMEM((3, *LINE), BF), STAGE, pltpu.SemaphoreType.DMA((3,))],
        compiler_params=ROOMY,
        name="pack_lines",
    )(*ins)


def body(queries, attn_keys, attn_values, out_proj, grad_out, plane_axes):
    swap = [(0, 1), (1, 0)]
    q, k, v = queries[0], attn_keys[0], attn_values[0]

    cotangent = grad_out.reshape(TOKENS)
    other = lax.ppermute(cotangent, "head", swap)
    lines = exchange(pack_lines(q, k, v), SENT)
    ga, top, total, own_out = own(cotangent, other, out_proj, q, k, v)

    sent, q6, k6, v6, near_out, far_out, totals = forward(
        plane_axes, q, k, v, ga, top, total, own_out, lines
    )
    mixed = exchange(sent, MIXED)
    ga_columns, log_all, delta, given, kept = merge(ga, near_out, far_out, totals, out_proj, mixed)
    arrived = lax.ppermute(given, "head", swap)
    dq, dk, dv, sent = backward(
        plane_axes, q6, k6, v6, ga, ga_columns, log_all, delta
    )
    returned = exchange(sent, SENT)
    layer = call(
        layer_kernel, (kept, arrived), [shape(*TOKENS)], [], "layer", estimate=cost(LONG, 1500000)
    )
    dq, dk, dv = finish(dq, dk, dv, returned)
    return layer.reshape(1, 3, HALF, 1024), dq[None], dk[None], dv[None]


def solution(mesh):
    lines = P("band", None, None, "head")
    columns = P("band", None, "head", None)
    return jax.shard_map(
        body,
        mesh=mesh,
        in_specs=(lines, lines, lines, P("head", None), columns, P()),
        out_specs=(columns, lines, lines, lines),
        check_vma=False,
    )
```

```python
import jax
import jax.numpy as jnp
from jax import lax
from jax.experimental import pallas as pl
from jax.experimental.pallas import tpu as pltpu
from jax.sharding import PartitionSpec as P

BF = jnp.bfloat16
F32 = jnp.float32
N = 128
HALF = 64
SENT = 18
MIXED = 14
UNROLL = True
FACTOR = 0.125
LONG = 60 * 10**9
PARAMS = pltpu.CompilerParams(vmem_limit_bytes=48 * 1024 * 1024)
ROOMY = pltpu.CompilerParams(vmem_limit_bytes=60 * 1024 * 1024)
VMEM = pl.BlockSpec(memory_space=pltpu.VMEM)
HBM = pl.BlockSpec(memory_space=pltpu.HBM)
SMEM = pl.BlockSpec(memory_space=pltpu.SMEM)


def nt(a, b):
    return lax.dot_general(a, b, (((1,), (1,)), ((), ())), preferred_element_type=F32)


def tn(a, b):
    return lax.dot_general(a, b, (((0,), (0,)), ((), ())), preferred_element_type=F32)


def nn(a, b):
    return lax.dot_general(a, b, (((1,), (0,)), ((), ())), preferred_element_type=F32)


def lane_masks():
    lane = lax.broadcasted_iota(jnp.int32, (N, N), 1)
    first = jnp.where(lane < HALF, 1.0, 0.0)
    return first.astype(BF), (1.0 - first).astype(BF)


def stack(x, masks):
    return jnp.concatenate([x * masks[0], x * masks[1]], axis=0)


def head_sums(product):
    row = lax.broadcasted_iota(jnp.int32, (8, 256), 0)
    lane = lax.broadcasted_iota(jnp.int32, (8, 256), 1)
    pick = jnp.where(lane // HALF == row, 1.0, 0.0).astype(BF)
    high = product.astype(BF)
    low = (product - high.astype(F32)).astype(BF)
    return nt(pick, high) + nt(pick, low)


def partner_of(axes_ref, b):
    axis = axes_ref[lax.rem(b, 3), lax.div(b, 3)]
    found = jnp.int32(0)
    for c in range(6):
        same = jnp.logical_and(axes_ref[c % 3, c // 3] == axis, b != c)
        found = found + jnp.where(same, jnp.int32(c), jnp.int32(0))
    return found


def planes(step):
    lax.fori_loop(0, 3, lambda p, _: (step(p), 0)[1], 0, unroll=UNROLL)


def tall(x):
    return jnp.concatenate([x[:, :N], x[:, N:]], axis=0)


def wide(rows, r):
    return jnp.concatenate([rows[r : r + 1], rows[r + 1 : r + 2]], axis=1)


def spread(columns, r):
    lane = lax.broadcasted_iota(jnp.int32, (N, N), 1)
    return jnp.where(lane < HALF, columns[:, r : r + 1], columns[:, r + 1 : r + 2])


def pack_lines_kernel(q_ref, k_ref, v_ref, out_ref, held, stage, packed, in_sems, out_sems):
    def arriving(a, ref, h):
        cols = slice(HALF * h, HALF * h + HALF)
        return pltpu.make_async_copy(ref.at[:, cols, :], held.at[a, :, cols, :], in_sems.at[a, h])

    def leaving(h):
        rows = pl.ds(HALF * SENT * h, HALF * SENT)
        return pltpu.make_async_copy(packed.at[rows], out_ref.at[rows], out_sems.at[h])

    inputs = (q_ref, k_ref, v_ref)
    for h in range(2):
        for a, ref in enumerate(inputs):
            arriving(a, ref, h).start()
    for h in range(2):
        cols = slice(HALF * h, HALF * h + HALF)
        for a, ref in enumerate(inputs):
            arriving(a, ref, h).wait()
            for p in range(3):
                for g in range(2):
                    rows = pl.ds(HALF * SENT * h + 2 * (3 * a + p) + g, HALF, stride=SENT)
                    stage[rows, :] = held[a, p, cols, N * g : N * g + N].astype(F32)
        rows = slice(HALF * SENT * h, HALF * SENT * h + HALF * SENT)
        packed[rows, :] = stage[rows, :].astype(BF)
        leaving(h).start()
    for h in range(2):
        leaving(h).wait()


def own_kernel(
    own_ref, other_ref, proj_ref, q_ref, k_ref, v_ref,
    ga_ref, top_ref, sum_ref, out_ref,
):
    me = lax.axis_index("head")
    for ref, side in ((own_ref, me), (other_ref, 1 - me)):
        made = nt(ref[...], proj_ref[...]).astype(BF)
        for p in range(3):
            ga_ref[p, pl.ds(pl.multiple_of(side * HALF, HALF), HALF), :] = made[
                HALF * p : HALF * p + HALF
            ]
    masks = lane_masks()

    def step(p):
        for g in range(2):
            lanes = slice(N * g, N * g + N)
            scores = nt(k_ref[p, :, lanes], stack(q_ref[p, :, lanes] * BF(FACTOR), masks))
            top = jnp.max(scores, axis=0, keepdims=True)
            raised = jnp.exp(scores - top)
            top_ref[p, g] = top
            sum_ref[p, g] = jnp.sum(raised, axis=0, keepdims=True)
            out_ref[p, :, lanes] = tn(tall(raised.astype(BF)), stack(v_ref[p, :, lanes], masks))

    planes(step)


def forward_kernel(
    axes_ref, q_ref, k_ref, v_ref, ga_ref, top_ref, sum_ref, own_ref, got_ref,
    send_ref, q6, k6, v6, near_ref, far_ref, totals_ref,
    stage, parts, rows, probs,
):
    masks = lane_masks()
    stage[...] = got_ref[...].astype(F32)
    for a, (mine, six) in enumerate(((q_ref, q6), (k_ref, k6), (v_ref, v6))):
        for p in range(3):
            six[p] = mine[p]
            for g in range(2):
                lines = pl.ds(2 * (3 * a + p) + g, N, stride=SENT)
                six[3 + p, :, N * g : N * g + N] = stage[lines, :].astype(BF)

    blocks = [(b, partner_of(axes_ref, b)) for b in range(6)]
    for g in range(2):
        lanes = slice(N * g, N * g + N)
        for b, c in blocks:
            p = b % 3
            scores = nt(k6[c, :, lanes], stack(q6[b, :, lanes] * BF(FACTOR), masks))
            top = jnp.max(scores, axis=0, keepdims=True)
            if b < 3:
                top = jnp.maximum(top, top_ref[p, g])
                before = jnp.exp(top_ref[p, g] - top)
            raised = jnp.exp(scores - top)
            total = jnp.sum(raised, axis=0, keepdims=True)
            if b < 3:
                total = total + sum_ref[p, g] * before
            scale = 1.0 / total
            probs[2 * b + g] = (raised * scale).astype(BF)
            rows[b // 3, p, g] = top + jnp.log(total)
            if b < 3:
                rows[2, p, g] = before * scale
    for g in range(2):
        lanes = slice(N * g, N * g + N)
        for b, c in blocks:
            out = tn(tall(probs[2 * b + g]), stack(v6[c, :, lanes], masks))
            if b < 3:
                near_ref[b, :, lanes] = out
            else:
                far_ref[b - 3, :, lanes] = out.astype(BF)
    totals_ref[...] = jnp.zeros((40, N), F32)
    parts[...] = jnp.zeros((N, N), F32)
    for p in range(3):
        for g in range(2):
            for h in range(2):
                r = 4 * p + 2 * g + h
                half = slice(N * h, N * h + N)
                totals_ref[r : r + 1, :] = rows[0, p, g, :, half]
                totals_ref[24 + r : 25 + r, :] = rows[1, p, g, :, half]
                parts[r : r + 1, :] = rows[2, p, g, :, half]
    weights = jnp.transpose(parts[...])
    for p in range(3):
        for g in range(2):
            lanes = slice(N * g, N * g + N)
            near_ref[p, :, lanes] += spread(weights, 4 * p + 2 * g) * own_ref[p, :, lanes]
        totals_ref[12 + 4 * p : 16 + 4 * p, :] = head_sums(
            ga_ref[p].astype(F32) * near_ref[p]
        )[:4]
    left = totals_ref[...]
    for piece in range(3):
        rounded = left.astype(BF).astype(F32)
        parts[40 * piece : 40 * piece + 40, :] = rounded
        left = left - rounded
    stage[pl.ds(12, N, stride=MIXED), :] = jnp.transpose(parts[...])
    stage[pl.ds(13, N, stride=MIXED), :] = jnp.zeros((N, N), F32)
    for p in range(3):
        for g in range(2):
            lanes = slice(N * g, N * g + N)
            stage[pl.ds(2 * p + g, N, stride=MIXED), :] = far_ref[p, :, lanes].astype(F32)
            stage[pl.ds(6 + 2 * p + g, N, stride=MIXED), :] = ga_ref[p, :, lanes].astype(F32)
    send_ref[...] = stage[: MIXED * N, :].astype(BF)


def both_weights(near, far):
    top = jnp.maximum(near, far)
    log_all = top + jnp.log(jnp.exp(near - top) + jnp.exp(far - top))
    return log_all, jnp.exp(near - log_all), jnp.exp(far - log_all)


def merge_kernel(
    ga_ref, near_ref, far_ref, totals_ref, proj_ref, got_ref,
    ga_col_ref, log_all_ref, delta_ref, given_ref, kept_ref,
    stage, parts, att,
):
    stage[...] = got_ref[...].astype(F32)
    parts[...] = jnp.transpose(stage[pl.ds(12, N, stride=MIXED), :])
    arrived = parts[0:40, :] + (parts[40:80, :] + parts[80:120, :])
    for p in range(3):
        for g in range(2):
            ga_col_ref[p, :, N * g : N * g + N] = stage[
                pl.ds(6 + 2 * p + g, N, stride=MIXED), :
            ].astype(BF)
    row_log, row_near, row_far = both_weights(totals_ref[0:12, :], arrived[24:36])
    col_log, col_near, col_far = both_weights(arrived[0:12], totals_ref[24:36, :])
    row_delta = row_near * totals_ref[12:24, :]
    col_delta = col_near * arrived[12:24]
    for p in range(3):
        far_row = jnp.concatenate(
            [stage[pl.ds(2 * p + g, N, stride=MIXED), :] for g in range(2)], axis=1
        )
        heads = slice(4 * p, 4 * p + 4)
        row_sums = head_sums(ga_ref[p].astype(F32) * far_row)[:4]
        col_sums = head_sums(ga_col_ref[p].astype(F32) * far_ref[p].astype(F32))[:4]
        row = row_delta[heads] + row_far[heads] * row_sums
        col = col_delta[heads] + col_far[heads] * col_sums
        for g in range(2):
            log_all_ref[p, g] = wide(row_log, 4 * p + 2 * g)
            log_all_ref[3 + p, g] = wide(col_log, 4 * p + 2 * g)
            delta_ref[p, g] = wide(row, 2 * g)
            delta_ref[3 + p, g] = wide(col, 2 * g)
    parts[0:12, :] = row_near
    parts[12:24, :] = row_far
    weights = jnp.transpose(parts[...])
    for p in range(3):
        for g in range(2):
            r = 4 * p + 2 * g
            att[p, :, N * g : N * g + N] = (
                spread(weights, r) * near_ref[p, :, N * g : N * g + N]
                + spread(weights, 12 + r) * stage[pl.ds(2 * p + g, N, stride=MIXED), :]
            ).astype(BF)
    me = lax.axis_index("head")
    theirs = pl.ds(pl.multiple_of((1 - me) * HALF, HALF), HALF)
    mine = pl.ds(pl.multiple_of(me * HALF, HALF), HALF)
    for p in range(3):
        rows = slice(HALF * p, HALF * p + HALF)
        kept_ref[rows, :] = att[p, mine, :]
        given_ref[rows, :] = nn(att[p, theirs, :], proj_ref[...]).astype(BF)


def layer_kernel(kept_ref, proj_ref, got_ref, out_ref):
    out_ref[...] = (nn(kept_ref[...], proj_ref[...]) + got_ref[...].astype(F32)).astype(BF)


def backward_kernel(
    axes_ref, q6, k6, v6, ga_ref, ga_col_ref, log_all_ref, delta_ref,
    dq_ref, dk_ref, dv_ref, send_ref,
    stage, ga6, dq6, probs, steps, packed, sem,
):
    masks = lane_masks()

    def operands(b, g):
        lanes = slice(N * g, N * g + N)
        return stack(q6[b, :, lanes] * BF(FACTOR), masks), stack(ga6[b, :, lanes], masks)

    for p in range(3):
        ga6[p] = ga_ref[p]
        ga6[p + 3] = ga_col_ref[p]

    def score(units):
        for g in range(2):
            lanes = slice(N * g, N * g + N)
            for u, b, c in units:
                queries, grads = operands(b, g)
                prob = jnp.exp(nt(k6[c, :, lanes], queries) - log_all_ref[b, g]).astype(BF)
                dots = nt(v6[c, :, lanes], grads)
                probs[2 * u + g] = prob
                steps[2 * u + g] = (prob.astype(F32) * (dots - delta_ref[b, g])).astype(BF)

    def multiply(g, u, b, c):
        queries, grads = operands(b, g)
        step = steps[2 * u + g]
        dq = tn(tall(step), stack(k6[c, :, N * g : N * g + N], masks))
        return dq, nn(step, queries), nn(probs[2 * u + g], grads)

    cross = [(c, partner_of(axes_ref, c), c) for c in range(6)]
    same = [(c, c, c) for c in range(3)]
    score(cross)
    for g in range(2):
        lanes = slice(N * g, N * g + N)
        for u, b, c in cross:
            dq, dk, dv = multiply(g, u, b, c)
            dq6[b, :, lanes] = dq
            if c < 3:
                dk_ref[c, :, lanes] = dk
                dv_ref[c, :, lanes] = dv
            else:
                stage[pl.ds(2 * c + g, N, stride=SENT), :] = dk
                stage[pl.ds(6 + 2 * c + g, N, stride=SENT), :] = dv
    for p in range(3):
        for g in range(2):
            lanes = slice(N * g, N * g + N)
            stage[pl.ds(2 * p + g, N, stride=SENT), :] = dq6[3 + p, :, lanes] * FACTOR
    packed[...] = stage[...].astype(BF)
    leaving = pltpu.make_async_copy(packed, send_ref, sem)
    leaving.start()
    score(same)
    for g in range(2):
        lanes = slice(N * g, N * g + N)
        for u, b, c in same:
            dq, dk, dv = multiply(g, u, b, c)
            dq_ref[c, :, lanes] = (dq6[c, :, lanes] + dq) * FACTOR
            dk_ref[c, :, lanes] += dk
            dv_ref[c, :, lanes] += dv
    leaving.wait()


def finish_kernel(dq_ref, dk_ref, dv_ref, got_ref, q_out, k_out, v_out, stage, made, sems):
    stage[...] = got_ref[...].astype(F32)
    copies = []
    for a, (mine, out) in enumerate(((dq_ref, q_out), (dk_ref, k_out), (dv_ref, v_out))):
        for p in range(3):
            for g in range(2):
                lanes = slice(N * g, N * g + N)
                rows = pl.ds(2 * (3 * a + p) + g, N, stride=SENT)
                made[a, p, :, lanes] = (mine[p, :, lanes] + stage[rows, :]).astype(BF)
        copies.append(pltpu.make_async_copy(made.at[a], out, sems.at[a]))
        copies[-1].start()
    for copy in copies:
        copy.wait()


def shape(*dims, dtype=BF):
    return jax.ShapeDtypeStruct(dims, dtype)


def cost(flops, moved):
    return pl.CostEstimate(flops=flops, bytes_accessed=moved, transcendentals=0)


def exchange(sent, rows):
    sent = sent.reshape(N, rows // 2, 2, N)
    got = lax.all_to_all(sent, "band", split_axis=0, concat_axis=0, tiled=True)
    return got.reshape(N * rows, N)


LINE = (3, N, 256)
TOKENS = (3 * HALF, 1024)
PAIR = (3, 2, N, 256)
ROW = (3, 2, 1, 256)
STAGE = pltpu.VMEM((SENT * N, N), F32)
PACKED = pltpu.VMEM((SENT * N, N), BF)
SQUARE = pltpu.VMEM((N, N), F32)


def call(kernel, ins, outs, scratch, name, params=PARAMS, estimate=None):
    many = len(outs) > 1
    return pl.pallas_call(
        kernel,
        out_shape=tuple(outs) if many else outs[0],
        in_specs=[SMEM if x.dtype == jnp.int32 else VMEM for x in ins],
        out_specs=(VMEM,) * len(outs) if many else VMEM,
        scratch_shapes=scratch,
        compiler_params=params,
        cost_estimate=estimate,
        name=name,
    )(*ins)


def own(*ins):
    outs = [shape(*LINE), shape(*ROW, dtype=F32), shape(*ROW, dtype=F32), shape(*LINE, dtype=F32)]
    return call(own_kernel, ins, outs, [], "own", estimate=cost(LONG, 3000000))


def forward(*ins):
    outs = [shape(MIXED * N, N)] + [shape(6, N, 256)] * 3
    outs += [shape(*LINE, dtype=F32), shape(*LINE), shape(40, N, dtype=F32)]
    return call(forward_kernel, ins, outs, [STAGE, SQUARE, pltpu.VMEM((3, *ROW), F32), pltpu.VMEM((12, N, 256), BF)], "forward")


def merge(*ins):
    rows = shape(6, 2, 1, 256, dtype=F32)
    outs = [shape(*LINE), rows, rows, shape(*TOKENS), shape(3 * HALF, 256)]
    scratch = [pltpu.VMEM((MIXED * N, N), F32), SQUARE, pltpu.VMEM(LINE, BF)]
    return call(merge_kernel, ins, outs, scratch, "merge")


def backward(*ins):
    scratch = [STAGE, pltpu.VMEM((6, N, 256), BF), pltpu.VMEM((6, N, 256), F32)]
    scratch += [pltpu.VMEM((12, N, 256), BF)] * 2 + [PACKED, pltpu.SemaphoreType.DMA]
    return pl.pallas_call(
        backward_kernel,
        out_shape=(shape(*LINE, dtype=F32),) * 3 + (shape(SENT * N, N),),
        in_specs=[SMEM] + [VMEM] * (len(ins) - 1),
        out_specs=(VMEM, VMEM, VMEM, HBM),
        scratch_shapes=scratch,
        compiler_params=PARAMS,
        name="backward",
    )(*ins)


def finish(*ins):
    return pl.pallas_call(
        finish_kernel,
        out_shape=(shape(*LINE),) * 3,
        in_specs=[VMEM] * 4,
        out_specs=(HBM,) * 3,
        scratch_shapes=[STAGE, pltpu.VMEM((3, *LINE), BF), pltpu.SemaphoreType.DMA((3,))],
        compiler_params=PARAMS,
        name="finish",
    )(*ins)


def pack_lines(*ins):
    return pl.pallas_call(
        pack_lines_kernel,
        out_shape=shape(SENT * N, N),
        in_specs=[HBM] * 3,
        out_specs=HBM,
        scratch_shapes=[
            pltpu.VMEM((3, *LINE), BF),
            STAGE,
            PACKED,
            pltpu.SemaphoreType.DMA((3, 2)),
            pltpu.SemaphoreType.DMA((2,)),
        ],
        compiler_params=ROOMY,
        name="pack_lines",
    )(*ins)


def body(queries, attn_keys, attn_values, out_proj, grad_out, plane_axes):
    swap = [(0, 1), (1, 0)]
    q, k, v = queries[0], attn_keys[0], attn_values[0]

    cotangent = grad_out.reshape(TOKENS)
    other = lax.ppermute(cotangent, "head", swap)
    lines = exchange(pack_lines(q, k, v), SENT)
    ga, top, total, own_out = own(cotangent, other, out_proj, q, k, v)

    sent, q6, k6, v6, near_out, far_out, totals = forward(
        plane_axes, q, k, v, ga, top, total, own_out, lines
    )
    mixed = exchange(sent, MIXED)
    ga_columns, log_all, delta, given, kept = merge(ga, near_out, far_out, totals, out_proj, mixed)
    arrived = lax.ppermute(given, "head", swap)
    dq, dk, dv, sent = backward(
        plane_axes, q6, k6, v6, ga, ga_columns, log_all, delta
    )
    returned = exchange(sent, SENT)
    layer = call(
        layer_kernel, (kept, out_proj, arrived), [shape(*TOKENS)], [], "layer", estimate=cost(LONG, 1500000)
    )
    dq, dk, dv = finish(dq, dk, dv, returned)
    return layer.reshape(1, 3, HALF, 1024), dq[None], dk[None], dv[None]


def solution(mesh):
    lines = P("band", None, None, "head")
    columns = P("band", None, "head", None)
    return jax.shard_map(
        body,
        mesh=mesh,
        in_specs=(lines, lines, lines, P("head", None), columns, P()),
        out_specs=(columns, lines, lines, lines),
        check_vma=False,
    )
```

```python
import jax
import jax.numpy as jnp
from jax import lax
from jax.experimental import pallas as pl
from jax.experimental.pallas import tpu as pltpu
from jax.sharding import PartitionSpec as P

BF = jnp.bfloat16
F32 = jnp.float32
N = 128
HALF = 64
SENT = 18
MIXED = 14
UNROLL = True
FACTOR = 0.125
LONG = 60 * 10**9
PARAMS = pltpu.CompilerParams(vmem_limit_bytes=48 * 1024 * 1024)
ROOMY = pltpu.CompilerParams(vmem_limit_bytes=60 * 1024 * 1024)
VMEM = pl.BlockSpec(memory_space=pltpu.VMEM)
HBM = pl.BlockSpec(memory_space=pltpu.HBM)


def nt(a, b):
    return lax.dot_general(a, b, (((1,), (1,)), ((), ())), preferred_element_type=F32)


def tn(a, b):
    return lax.dot_general(a, b, (((0,), (0,)), ((), ())), preferred_element_type=F32)


def nn(a, b):
    return lax.dot_general(a, b, (((1,), (0,)), ((), ())), preferred_element_type=F32)


def lane_masks():
    lane = lax.broadcasted_iota(jnp.int32, (N, N), 1)
    first = jnp.where(lane < HALF, 1.0, 0.0)
    return first.astype(BF), (1.0 - first).astype(BF)


def stack(x, masks):
    return jnp.concatenate([x * masks[0], x * masks[1]], axis=0)


def head_sums(product):
    row = lax.broadcasted_iota(jnp.int32, (8, 256), 0)
    lane = lax.broadcasted_iota(jnp.int32, (8, 256), 1)
    pick = jnp.where(lane // HALF == row, 1.0, 0.0).astype(BF)
    high = product.astype(BF)
    low = (product - high.astype(F32)).astype(BF)
    return nt(pick, high) + nt(pick, low)


def partners(axes_ref):
    axes = axes_ref[...]
    axis = [axes[b % 3, b // 3] for b in range(6)]
    found = []
    for b in range(6):
        other = jnp.int32(0)
        for c in range(6):
            if c != b:
                other = other + jnp.where(axis[c] == axis[b], jnp.int32(c), jnp.int32(0))
        found.append(other)
    return found


def planes(step):
    lax.fori_loop(0, 3, lambda p, _: (step(p), 0)[1], 0, unroll=UNROLL)


def tall(x):
    return jnp.concatenate([x[:, :N], x[:, N:]], axis=0)


def wide(rows, r):
    return jnp.concatenate([rows[r : r + 1], rows[r + 1 : r + 2]], axis=1)


def spread(columns, r):
    lane = lax.broadcasted_iota(jnp.int32, (N, N), 1)
    return jnp.where(lane < HALF, columns[:, r : r + 1], columns[:, r + 1 : r + 2])


def pack_lines_kernel(q_ref, k_ref, v_ref, out_ref, held, stage, packed, in_sems, out_sems):
    def arriving(a, ref, h):
        cols = slice(HALF * h, HALF * h + HALF)
        return pltpu.make_async_copy(ref.at[:, cols, :], held.at[a, :, cols, :], in_sems.at[a, h])

    def leaving(h):
        rows = pl.ds(HALF * SENT * h, HALF * SENT)
        return pltpu.make_async_copy(packed.at[rows], out_ref.at[rows], out_sems.at[h])

    inputs = (q_ref, k_ref, v_ref)
    for h in range(2):
        for a, ref in enumerate(inputs):
            arriving(a, ref, h).start()
    for h in range(2):
        cols = slice(HALF * h, HALF * h + HALF)
        for a, ref in enumerate(inputs):
            arriving(a, ref, h).wait()
            for p in range(3):
                for g in range(2):
                    rows = pl.ds(HALF * SENT * h + 2 * (3 * a + p) + g, HALF, stride=SENT)
                    stage[rows, :] = held[a, p, cols, N * g : N * g + N].astype(F32)
        rows = slice(HALF * SENT * h, HALF * SENT * h + HALF * SENT)
        packed[rows, :] = stage[rows, :].astype(BF)
        leaving(h).start()
    for h in range(2):
        leaving(h).wait()


def own_kernel(
    own_ref, other_ref, proj_ref, q_ref, k_ref, v_ref,
    ga_ref, top_ref, sum_ref, out_ref,
):
    me = lax.axis_index("head")
    for ref, side in ((own_ref, me), (other_ref, 1 - me)):
        made = nt(ref[...], proj_ref[...]).astype(BF)
        for p in range(3):
            ga_ref[p, pl.ds(pl.multiple_of(side * HALF, HALF), HALF), :] = made[
                HALF * p : HALF * p + HALF
            ]
    masks = lane_masks()

    def step(p):
        for g in range(2):
            lanes = slice(N * g, N * g + N)
            scores = nt(k_ref[p, :, lanes], stack(q_ref[p, :, lanes] * BF(FACTOR), masks))
            top = jnp.max(scores, axis=0, keepdims=True)
            raised = jnp.exp(scores - top)
            top_ref[p, g] = top
            sum_ref[p, g] = jnp.sum(raised, axis=0, keepdims=True)
            out_ref[p, :, lanes] = tn(tall(raised.astype(BF)), stack(v_ref[p, :, lanes], masks))

    planes(step)


def forward_kernel(
    axes_ref, q_ref, k_ref, v_ref, ga_ref, top_ref, sum_ref, own_ref, got_ref,
    send_ref, q6, k6, v6, near_ref, far_ref, totals_ref,
    stage, parts, rows, probs,
):
    masks = lane_masks()
    stage[...] = got_ref[...].astype(F32)
    for a, (mine, six) in enumerate(((q_ref, q6), (k_ref, k6), (v_ref, v6))):
        for p in range(3):
            six[p] = mine[p]
            for g in range(2):
                lines = pl.ds(2 * (3 * a + p) + g, N, stride=SENT)
                six[3 + p, :, N * g : N * g + N] = stage[lines, :].astype(BF)

    blocks = list(enumerate(partners(axes_ref)))
    for g in range(2):
        lanes = slice(N * g, N * g + N)
        for b, c in blocks:
            p = b % 3
            scores = nt(k6[c, :, lanes], stack(q6[b, :, lanes] * BF(FACTOR), masks))
            top = jnp.max(scores, axis=0, keepdims=True)
            if b < 3:
                top = jnp.maximum(top, top_ref[p, g])
                before = jnp.exp(top_ref[p, g] - top)
            raised = jnp.exp(scores - top)
            total = jnp.sum(raised, axis=0, keepdims=True)
            if b < 3:
                total = total + sum_ref[p, g] * before
            scale = 1.0 / total
            probs[2 * b + g] = (raised * scale).astype(BF)
            rows[b // 3, p, g] = top + jnp.log(total)
            if b < 3:
                rows[2, p, g] = before * scale
    for g in range(2):
        lanes = slice(N * g, N * g + N)
        for b, c in blocks:
            out = tn(tall(probs[2 * b + g]), stack(v6[c, :, lanes], masks))
            if b < 3:
                near_ref[b, :, lanes] = out
            else:
                far_ref[b - 3, :, lanes] = out.astype(BF)
    totals_ref[...] = jnp.zeros((40, N), F32)
    parts[...] = jnp.zeros((N, N), F32)
    for p in range(3):
        for g in range(2):
            for h in range(2):
                r = 4 * p + 2 * g + h
                half = slice(N * h, N * h + N)
                totals_ref[r : r + 1, :] = rows[0, p, g, :, half]
                totals_ref[24 + r : 25 + r, :] = rows[1, p, g, :, half]
                parts[r : r + 1, :] = rows[2, p, g, :, half]
    weights = jnp.transpose(parts[...])
    for p in range(3):
        for g in range(2):
            lanes = slice(N * g, N * g + N)
            near_ref[p, :, lanes] += spread(weights, 4 * p + 2 * g) * own_ref[p, :, lanes]
        totals_ref[12 + 4 * p : 16 + 4 * p, :] = head_sums(
            ga_ref[p].astype(F32) * near_ref[p]
        )[:4]
    left = totals_ref[...]
    for piece in range(3):
        rounded = left.astype(BF).astype(F32)
        parts[40 * piece : 40 * piece + 40, :] = rounded
        left = left - rounded
    stage[pl.ds(12, N, stride=MIXED), :] = jnp.transpose(parts[...])
    stage[pl.ds(13, N, stride=MIXED), :] = jnp.zeros((N, N), F32)
    for p in range(3):
        for g in range(2):
            lanes = slice(N * g, N * g + N)
            stage[pl.ds(2 * p + g, N, stride=MIXED), :] = far_ref[p, :, lanes].astype(F32)
            stage[pl.ds(6 + 2 * p + g, N, stride=MIXED), :] = ga_ref[p, :, lanes].astype(F32)
    send_ref[...] = stage[: MIXED * N, :].astype(BF)


def both_weights(near, far):
    top = jnp.maximum(near, far)
    log_all = top + jnp.log(jnp.exp(near - top) + jnp.exp(far - top))
    return log_all, jnp.exp(near - log_all), jnp.exp(far - log_all)


def merge_kernel(
    ga_ref, near_ref, far_ref, totals_ref, proj_ref, got_ref,
    ga_col_ref, log_all_ref, delta_ref, given_ref, kept_ref,
    stage, parts, att,
):
    stage[...] = got_ref[...].astype(F32)
    parts[...] = jnp.transpose(stage[pl.ds(12, N, stride=MIXED), :])
    arrived = parts[0:40, :] + (parts[40:80, :] + parts[80:120, :])
    for p in range(3):
        for g in range(2):
            ga_col_ref[p, :, N * g : N * g + N] = stage[
                pl.ds(6 + 2 * p + g, N, stride=MIXED), :
            ].astype(BF)
    row_log, row_near, row_far = both_weights(totals_ref[0:12, :], arrived[24:36])
    col_log, col_near, col_far = both_weights(arrived[0:12], totals_ref[24:36, :])
    row_delta = row_near * totals_ref[12:24, :]
    col_delta = col_near * arrived[12:24]
    for p in range(3):
        far_row = jnp.concatenate(
            [stage[pl.ds(2 * p + g, N, stride=MIXED), :] for g in range(2)], axis=1
        )
        heads = slice(4 * p, 4 * p + 4)
        row_sums = head_sums(ga_ref[p].astype(F32) * far_row)[:4]
        col_sums = head_sums(ga_col_ref[p].astype(F32) * far_ref[p].astype(F32))[:4]
        row = row_delta[heads] + row_far[heads] * row_sums
        col = col_delta[heads] + col_far[heads] * col_sums
        for g in range(2):
            log_all_ref[p, g] = wide(row_log, 4 * p + 2 * g)
            log_all_ref[3 + p, g] = wide(col_log, 4 * p + 2 * g)
            delta_ref[p, g] = wide(row, 2 * g)
            delta_ref[3 + p, g] = wide(col, 2 * g)
    parts[0:12, :] = row_near
    parts[12:24, :] = row_far
    weights = jnp.transpose(parts[...])
    for p in range(3):
        for g in range(2):
            r = 4 * p + 2 * g
            att[p, :, N * g : N * g + N] = (
                spread(weights, r) * near_ref[p, :, N * g : N * g + N]
                + spread(weights, 12 + r) * stage[pl.ds(2 * p + g, N, stride=MIXED), :]
            ).astype(BF)
    me = lax.axis_index("head")
    theirs = pl.ds(pl.multiple_of((1 - me) * HALF, HALF), HALF)
    mine = pl.ds(pl.multiple_of(me * HALF, HALF), HALF)
    for p in range(3):
        rows = slice(HALF * p, HALF * p + HALF)
        kept_ref[rows, :] = att[p, mine, :]
        given_ref[rows, :] = nn(att[p, theirs, :], proj_ref[...]).astype(BF)


def layer_kernel(kept_ref, proj_ref, got_ref, out_ref):
    out_ref[...] = (nn(kept_ref[...], proj_ref[...]) + got_ref[...].astype(F32)).astype(BF)


def backward_kernel(
    axes_ref, q6, k6, v6, ga_ref, ga_col_ref, log_all_ref, delta_ref,
    dq_ref, dk_ref, dv_ref, send_ref,
    stage, ga6, dq6, probs, steps, packed, sem,
):
    masks = lane_masks()

    def operands(b, g):
        lanes = slice(N * g, N * g + N)
        return stack(q6[b, :, lanes] * BF(FACTOR), masks), stack(ga6[b, :, lanes], masks)

    for p in range(3):
        ga6[p] = ga_ref[p]
        ga6[p + 3] = ga_col_ref[p]

    def score(units):
        for g in range(2):
            lanes = slice(N * g, N * g + N)
            for u, b, c in units:
                queries, grads = operands(b, g)
                prob = jnp.exp(nt(k6[c, :, lanes], queries) - log_all_ref[b, g])
                dots = nt(v6[c, :, lanes], grads)
                probs[2 * u + g] = prob.astype(BF)
                steps[2 * u + g] = (prob * (dots - delta_ref[b, g])).astype(BF)

    def multiply(g, u, b, c):
        queries, grads = operands(b, g)
        step = steps[2 * u + g]
        dq = tn(tall(step), stack(k6[c, :, N * g : N * g + N], masks))
        return dq, nn(step, queries), nn(probs[2 * u + g], grads)

    cross = [(c, b, c) for c, b in enumerate(partners(axes_ref))]
    same = [(c, c, c) for c in range(3)]
    score(cross)
    for g in range(2):
        lanes = slice(N * g, N * g + N)
        for u, b, c in cross:
            dq, dk, dv = multiply(g, u, b, c)
            dq6[b, :, lanes] = dq
            if c < 3:
                dk_ref[c, :, lanes] = dk
                dv_ref[c, :, lanes] = dv
            else:
                stage[pl.ds(2 * c + g, N, stride=SENT), :] = dk
                stage[pl.ds(6 + 2 * c + g, N, stride=SENT), :] = dv
    for p in range(3):
        for g in range(2):
            lanes = slice(N * g, N * g + N)
            stage[pl.ds(2 * p + g, N, stride=SENT), :] = dq6[3 + p, :, lanes] * FACTOR
    packed[...] = stage[...].astype(BF)
    leaving = pltpu.make_async_copy(packed, send_ref, sem)
    leaving.start()
    score(same)
    for g in range(2):
        lanes = slice(N * g, N * g + N)
        for u, b, c in same:
            dq, dk, dv = multiply(g, u, b, c)
            dq_ref[c, :, lanes] = (dq6[c, :, lanes] + dq) * FACTOR
            dk_ref[c, :, lanes] += dk
            dv_ref[c, :, lanes] += dv
    leaving.wait()


def finish_kernel(dq_ref, dk_ref, dv_ref, got_ref, q_out, k_out, v_out, stage, made, sems):
    stage[...] = got_ref[...].astype(F32)
    copies = []
    for a, (mine, out) in enumerate(((dq_ref, q_out), (dk_ref, k_out), (dv_ref, v_out))):
        for p in range(3):
            for g in range(2):
                lanes = slice(N * g, N * g + N)
                rows = pl.ds(2 * (3 * a + p) + g, N, stride=SENT)
                made[a, p, :, lanes] = (mine[p, :, lanes] + stage[rows, :]).astype(BF)
        copies.append(pltpu.make_async_copy(made.at[a], out, sems.at[a]))
        copies[-1].start()
    for copy in copies:
        copy.wait()


def shape(*dims, dtype=BF):
    return jax.ShapeDtypeStruct(dims, dtype)


def cost(flops, moved):
    return pl.CostEstimate(flops=flops, bytes_accessed=moved, transcendentals=0)


def exchange(sent, rows):
    sent = sent.reshape(N, rows // 2, 2, N)
    got = lax.all_to_all(sent, "band", split_axis=0, concat_axis=0, tiled=True)
    return got.reshape(N * rows, N)


LINE = (3, N, 256)
TOKENS = (3 * HALF, 1024)
PAIR = (3, 2, N, 256)
ROW = (3, 2, 1, 256)
STAGE = pltpu.VMEM((SENT * N, N), F32)
PACKED = pltpu.VMEM((SENT * N, N), BF)
SQUARE = pltpu.VMEM((N, N), F32)


def call(kernel, ins, outs, scratch, name, params=PARAMS, estimate=None):
    many = len(outs) > 1
    return pl.pallas_call(
        kernel,
        out_shape=tuple(outs) if many else outs[0],
        in_specs=[VMEM] * len(ins),
        out_specs=(VMEM,) * len(outs) if many else VMEM,
        scratch_shapes=scratch,
        compiler_params=params,
        cost_estimate=estimate,
        name=name,
    )(*ins)


def own(*ins):
    outs = [shape(*LINE), shape(*ROW, dtype=F32), shape(*ROW, dtype=F32), shape(*LINE, dtype=F32)]
    return call(own_kernel, ins, outs, [], "own", estimate=cost(LONG, 3000000))


def forward(*ins):
    outs = [shape(MIXED * N, N)] + [shape(6, N, 256)] * 3
    outs += [shape(*LINE, dtype=F32), shape(*LINE), shape(40, N, dtype=F32)]
    return call(forward_kernel, ins, outs, [STAGE, SQUARE, pltpu.VMEM((3, *ROW), F32), pltpu.VMEM((12, N, 256), BF)], "forward")


def merge(*ins):
    rows = shape(6, 2, 1, 256, dtype=F32)
    outs = [shape(*LINE), rows, rows, shape(*TOKENS), shape(3 * HALF, 256)]
    scratch = [pltpu.VMEM((MIXED * N, N), F32), SQUARE, pltpu.VMEM(LINE, BF)]
    return call(merge_kernel, ins, outs, scratch, "merge")


def backward(*ins):
    scratch = [STAGE, pltpu.VMEM((6, N, 256), BF), pltpu.VMEM((6, N, 256), F32)]
    scratch += [pltpu.VMEM((12, N, 256), BF)] * 2 + [PACKED, pltpu.SemaphoreType.DMA]
    return pl.pallas_call(
        backward_kernel,
        out_shape=(shape(*LINE, dtype=F32),) * 3 + (shape(SENT * N, N),),
        in_specs=[VMEM] * len(ins),
        out_specs=(VMEM, VMEM, VMEM, HBM),
        scratch_shapes=scratch,
        compiler_params=PARAMS,
        name="backward",
    )(*ins)


def finish(*ins):
    return pl.pallas_call(
        finish_kernel,
        out_shape=(shape(*LINE),) * 3,
        in_specs=[VMEM] * 4,
        out_specs=(HBM,) * 3,
        scratch_shapes=[STAGE, pltpu.VMEM((3, *LINE), BF), pltpu.SemaphoreType.DMA((3,))],
        compiler_params=PARAMS,
        name="finish",
    )(*ins)


def pack_lines(*ins):
    return pl.pallas_call(
        pack_lines_kernel,
        out_shape=shape(SENT * N, N),
        in_specs=[HBM] * 3,
        out_specs=HBM,
        scratch_shapes=[
            pltpu.VMEM((3, *LINE), BF),
            STAGE,
            PACKED,
            pltpu.SemaphoreType.DMA((3, 2)),
            pltpu.SemaphoreType.DMA((2,)),
        ],
        compiler_params=ROOMY,
        name="pack_lines",
    )(*ins)


def body(queries, attn_keys, attn_values, out_proj, grad_out, plane_axes):
    swap = [(0, 1), (1, 0)]
    q, k, v = queries[0], attn_keys[0], attn_values[0]

    cotangent = grad_out.reshape(TOKENS)
    other = lax.ppermute(cotangent, "head", swap)
    lines = exchange(pack_lines(q, k, v), SENT)
    ga, top, total, own_out = own(cotangent, other, out_proj, q, k, v)

    sent, q6, k6, v6, near_out, far_out, totals = forward(
        plane_axes, q, k, v, ga, top, total, own_out, lines
    )
    mixed = exchange(sent, MIXED)
    ga_columns, log_all, delta, given, kept = merge(ga, near_out, far_out, totals, out_proj, mixed)
    arrived = lax.ppermute(given, "head", swap)
    dq, dk, dv, sent = backward(
        plane_axes, q6, k6, v6, ga, ga_columns, log_all, delta
    )
    returned = exchange(sent, SENT)
    layer = call(
        layer_kernel, (kept, out_proj, arrived), [shape(*TOKENS)], [], "layer", estimate=cost(LONG, 1500000)
    )
    dq, dk, dv = finish(dq, dk, dv, returned)
    return layer.reshape(1, 3, HALF, 1024), dq[None], dk[None], dv[None]


def solution(mesh):
    lines = P("band", None, None, "head")
    columns = P("band", None, "head", None)
    return jax.shard_map(
        body,
        mesh=mesh,
        in_specs=(lines, lines, lines, P("head", None), columns, P()),
        out_specs=(columns, lines, lines, lines),
        check_vma=False,
    )
```

```python
import jax
import jax.numpy as jnp
from jax import lax
from jax.experimental import pallas as pl
from jax.experimental.pallas import tpu as pltpu
from jax.sharding import PartitionSpec as P

BF = jnp.bfloat16
F32 = jnp.float32
N = 128
HALF = 64
SENT = 18
MIXED = 14
UNROLL = True
FACTOR = 0.125
LONG = 60 * 10**9
PARAMS = pltpu.CompilerParams(vmem_limit_bytes=48 * 1024 * 1024)
ROOMY = pltpu.CompilerParams(vmem_limit_bytes=60 * 1024 * 1024)
VMEM = pl.BlockSpec(memory_space=pltpu.VMEM)
HBM = pl.BlockSpec(memory_space=pltpu.HBM)


def nt(a, b):
    return lax.dot_general(a, b, (((1,), (1,)), ((), ())), preferred_element_type=F32)


def tn(a, b):
    return lax.dot_general(a, b, (((0,), (0,)), ((), ())), preferred_element_type=F32)


def nn(a, b):
    return lax.dot_general(a, b, (((1,), (0,)), ((), ())), preferred_element_type=F32)


def lane_masks():
    lane = lax.broadcasted_iota(jnp.int32, (N, N), 1)
    first = jnp.where(lane < HALF, 1.0, 0.0)
    return first.astype(BF), (1.0 - first).astype(BF)


def stack(x, masks):
    return jnp.concatenate([x * masks[0], x * masks[1]], axis=0)


def head_sums(product):
    row = lax.broadcasted_iota(jnp.int32, (8, 256), 0)
    lane = lax.broadcasted_iota(jnp.int32, (8, 256), 1)
    pick = jnp.where(lane // HALF == row, 1.0, 0.0).astype(BF)
    high = product.astype(BF)
    low = (product - high.astype(F32)).astype(BF)
    return nt(pick, high) + nt(pick, low)


def partners(axes_ref):
    axes = axes_ref[...]
    axis = [axes[b % 3, b // 3] for b in range(6)]
    found = []
    for b in range(6):
        other = jnp.int32(0)
        for c in range(6):
            if c != b:
                other = other + jnp.where(axis[c] == axis[b], jnp.int32(c), jnp.int32(0))
        found.append(other)
    return found


def planes(step):
    lax.fori_loop(0, 3, lambda p, _: (step(p), 0)[1], 0, unroll=UNROLL)


def tall(x):
    return jnp.concatenate([x[:, :N], x[:, N:]], axis=0)


def wide(rows, r):
    return jnp.concatenate([rows[r : r + 1], rows[r + 1 : r + 2]], axis=1)


def spread(columns, r):
    lane = lax.broadcasted_iota(jnp.int32, (N, N), 1)
    return jnp.where(lane < HALF, columns[:, r : r + 1], columns[:, r + 1 : r + 2])


def pack_lines_kernel(q_ref, k_ref, v_ref, out_ref, held, stage, packed, in_sems, out_sems):
    def arriving(a, ref, h):
        cols = slice(HALF * h, HALF * h + HALF)
        return pltpu.make_async_copy(ref.at[:, cols, :], held.at[a, :, cols, :], in_sems.at[a, h])

    def leaving(h):
        rows = pl.ds(HALF * SENT * h, HALF * SENT)
        return pltpu.make_async_copy(packed.at[rows], out_ref.at[rows], out_sems.at[h])

    inputs = (q_ref, k_ref, v_ref)
    for h in range(2):
        for a, ref in enumerate(inputs):
            arriving(a, ref, h).start()
    for h in range(2):
        cols = slice(HALF * h, HALF * h + HALF)
        for a, ref in enumerate(inputs):
            arriving(a, ref, h).wait()
            for p in range(3):
                for g in range(2):
                    rows = pl.ds(HALF * SENT * h + 2 * (3 * a + p) + g, HALF, stride=SENT)
                    stage[rows, :] = held[a, p, cols, N * g : N * g + N].astype(F32)
        rows = slice(HALF * SENT * h, HALF * SENT * h + HALF * SENT)
        packed[rows, :] = stage[rows, :].astype(BF)
        leaving(h).start()
    for h in range(2):
        leaving(h).wait()


def own_kernel(
    own_ref, other_ref, proj_ref, q_ref, k_ref, v_ref,
    ga_ref, top_ref, sum_ref, out_ref,
):
    me = lax.axis_index("head")
    for ref, side in ((own_ref, me), (other_ref, 1 - me)):
        made = nt(ref[...], proj_ref[...]).astype(BF)
        for p in range(3):
            ga_ref[p, pl.ds(pl.multiple_of(side * HALF, HALF), HALF), :] = made[
                HALF * p : HALF * p + HALF
            ]
    masks = lane_masks()

    def step(p):
        for g in range(2):
            lanes = slice(N * g, N * g + N)
            scores = nt(k_ref[p, :, lanes], stack(q_ref[p, :, lanes] * BF(FACTOR), masks))
            top = jnp.max(scores, axis=0, keepdims=True)
            raised = jnp.exp(scores - top)
            top_ref[p, g] = top
            sum_ref[p, g] = jnp.sum(raised, axis=0, keepdims=True)
            out_ref[p, :, lanes] = tn(tall(raised.astype(BF)), stack(v_ref[p, :, lanes], masks))

    planes(step)


def forward_kernel(
    axes_ref, q_ref, k_ref, v_ref, ga_ref, top_ref, sum_ref, own_ref, got_ref,
    send_ref, q6, k6, v6, near_ref, far_ref, totals_ref,
    stage, parts, rows, probs,
):
    masks = lane_masks()
    stage[...] = got_ref[...].astype(F32)
    for a, (mine, six) in enumerate(((q_ref, q6), (k_ref, k6), (v_ref, v6))):
        for p in range(3):
            six[p] = mine[p]
            for g in range(2):
                lines = pl.ds(2 * (3 * a + p) + g, N, stride=SENT)
                six[3 + p, :, N * g : N * g + N] = stage[lines, :].astype(BF)

    blocks = list(enumerate(partners(axes_ref)))
    for g in range(2):
        lanes = slice(N * g, N * g + N)
        for b, c in blocks:
            p = b % 3
            scores = nt(k6[c, :, lanes], stack(q6[b, :, lanes] * BF(FACTOR), masks))
            top = jnp.max(scores, axis=0, keepdims=True)
            if b < 3:
                top = jnp.maximum(top, top_ref[p, g])
                before = jnp.exp(top_ref[p, g] - top)
            raised = jnp.exp(scores - top)
            total = jnp.sum(raised, axis=0, keepdims=True)
            if b < 3:
                total = total + sum_ref[p, g] * before
            scale = 1.0 / total
            probs[2 * b + g] = (raised * scale).astype(BF)
            rows[b // 3, p, g] = top + jnp.log(total)
            if b < 3:
                rows[2, p, g] = before * scale
    for g in range(2):
        lanes = slice(N * g, N * g + N)
        for b, c in blocks:
            out = tn(tall(probs[2 * b + g]), stack(v6[c, :, lanes], masks))
            if b < 3:
                near_ref[b, :, lanes] = out
            else:
                far_ref[b - 3, :, lanes] = out.astype(BF)
    totals_ref[...] = jnp.zeros((40, N), F32)
    parts[...] = jnp.zeros((N, N), F32)
    for p in range(3):
        for g in range(2):
            for h in range(2):
                r = 4 * p + 2 * g + h
                half = slice(N * h, N * h + N)
                totals_ref[r : r + 1, :] = rows[0, p, g, :, half]
                totals_ref[24 + r : 25 + r, :] = rows[1, p, g, :, half]
                parts[r : r + 1, :] = rows[2, p, g, :, half]
    weights = jnp.transpose(parts[...])
    for p in range(3):
        for g in range(2):
            lanes = slice(N * g, N * g + N)
            near_ref[p, :, lanes] += spread(weights, 4 * p + 2 * g) * own_ref[p, :, lanes]
        totals_ref[12 + 4 * p : 16 + 4 * p, :] = head_sums(
            ga_ref[p].astype(F32) * near_ref[p]
        )[:4]
    left = totals_ref[...]
    for piece in range(3):
        rounded = left.astype(BF).astype(F32)
        parts[40 * piece : 40 * piece + 40, :] = rounded
        left = left - rounded
    stage[pl.ds(12, N, stride=MIXED), :] = jnp.transpose(parts[...])
    stage[pl.ds(13, N, stride=MIXED), :] = jnp.zeros((N, N), F32)
    for p in range(3):
        for g in range(2):
            lanes = slice(N * g, N * g + N)
            stage[pl.ds(2 * p + g, N, stride=MIXED), :] = far_ref[p, :, lanes].astype(F32)
            stage[pl.ds(6 + 2 * p + g, N, stride=MIXED), :] = ga_ref[p, :, lanes].astype(F32)
    send_ref[...] = stage[: MIXED * N, :].astype(BF)


def both_weights(near, far):
    top = jnp.maximum(near, far)
    log_all = top + jnp.log(jnp.exp(near - top) + jnp.exp(far - top))
    return log_all, jnp.exp(near - log_all), jnp.exp(far - log_all)


def score(queries, grads, keys, values, log_all, delta):
    prob = jnp.exp(nt(keys, queries) - log_all)
    return (prob * (nt(values, grads) - delta)).astype(BF), prob.astype(BF)


def multiply(queries, grads, keys, step, prob):
    return tn(tall(step), keys), nn(step, queries), nn(prob, grads)


def backward_kernel(
    axes_ref, q6, k6, v6, ga_ref, near_ref, far_ref, totals_ref, proj_ref, got_ref,
    dq_ref, dk_ref, dv_ref, send_ref, given_ref, kept_ref, log_row_ref, delta_row_ref,
    mixed, parts, att, log_all, delta, stage, ga6, dq6, probs, steps, packed, kept, sem, kept_sem,
):
    masks = lane_masks()
    mixed[...] = got_ref[...].astype(F32)
    parts[...] = jnp.transpose(mixed[pl.ds(12, N, stride=MIXED), :])
    arrived = parts[0:40, :] + (parts[40:80, :] + parts[80:120, :])
    for p in range(3):
        ga6[p] = ga_ref[p]
        for g in range(2):
            ga6[3 + p, :, N * g : N * g + N] = mixed[
                pl.ds(6 + 2 * p + g, N, stride=MIXED), :
            ].astype(BF)
    row_log, row_near, row_far = both_weights(totals_ref[0:12, :], arrived[24:36])
    col_log, col_near, col_far = both_weights(arrived[0:12], totals_ref[24:36, :])
    row_delta = row_near * totals_ref[12:24, :]
    col_delta = col_near * arrived[12:24]
    for p in range(3):
        far_row = jnp.concatenate(
            [mixed[pl.ds(2 * p + g, N, stride=MIXED), :] for g in range(2)], axis=1
        )
        heads = slice(4 * p, 4 * p + 4)
        row_sums = head_sums(ga_ref[p].astype(F32) * far_row)[:4]
        col_sums = head_sums(ga6[3 + p].astype(F32) * far_ref[p].astype(F32))[:4]
        row = row_delta[heads] + row_far[heads] * row_sums
        col = col_delta[heads] + col_far[heads] * col_sums
        for g in range(2):
            log_all[p, g] = wide(row_log, 4 * p + 2 * g)
            log_all[3 + p, g] = wide(col_log, 4 * p + 2 * g)
            delta[p, g] = wide(row, 2 * g)
            delta[3 + p, g] = wide(col, 2 * g)
    parts[0:12, :] = row_near
    parts[12:24, :] = row_far

    cross = list(enumerate(partners(axes_ref)))
    for g in range(2):
        lanes = slice(N * g, N * g + N)
        for c, b in cross:
            steps[2 * c + g], probs[2 * c + g] = score(
                stack(q6[b, :, lanes] * BF(FACTOR), masks),
                stack(ga6[b, :, lanes], masks),
                k6[c, :, lanes],
                v6[c, :, lanes],
                log_all[b, g],
                delta[b, g],
            )
    for g in range(2):
        lanes = slice(N * g, N * g + N)
        for c, b in cross:
            dq, dk, dv = multiply(
                stack(q6[b, :, lanes] * BF(FACTOR), masks),
                stack(ga6[b, :, lanes], masks),
                stack(k6[c, :, lanes], masks),
                steps[2 * c + g],
                probs[2 * c + g],
            )
            dq6[b, :, lanes] = dq
            if c < 3:
                dk_ref[c, :, lanes] = dk
                dv_ref[c, :, lanes] = dv
            else:
                stage[pl.ds(2 * c + g, N, stride=SENT), :] = dk
                stage[pl.ds(6 + 2 * c + g, N, stride=SENT), :] = dv
    for p in range(3):
        for g in range(2):
            lanes = slice(N * g, N * g + N)
            stage[pl.ds(2 * p + g, N, stride=SENT), :] = dq6[3 + p, :, lanes] * FACTOR
    packed[...] = stage[...].astype(BF)
    leaving = pltpu.make_async_copy(packed, send_ref, sem)
    leaving.start()

    weights = jnp.transpose(parts[...])
    for p in range(3):
        dq_ref[p] = dq6[p]
        log_row_ref[p] = log_all[p]
        delta_row_ref[p] = delta[p]
        for g in range(2):
            r = 4 * p + 2 * g
            att[p, :, N * g : N * g + N] = (
                spread(weights, r) * near_ref[p, :, N * g : N * g + N]
                + spread(weights, 12 + r) * mixed[pl.ds(2 * p + g, N, stride=MIXED), :]
            ).astype(BF)
    me = lax.axis_index("head")
    theirs = pl.ds(pl.multiple_of((1 - me) * HALF, HALF), HALF)
    mine = pl.ds(pl.multiple_of(me * HALF, HALF), HALF)
    for p in range(3):
        kept[HALF * p : HALF * p + HALF, :] = att[p, mine, :]
    keeping = pltpu.make_async_copy(kept, kept_ref, kept_sem)
    keeping.start()
    for p in range(3):
        given_ref[HALF * p : HALF * p + HALF, :] = nn(att[p, theirs, :], proj_ref[...]).astype(BF)
    keeping.wait()
    leaving.wait()


def rows_kernel(
    q_ref, k_ref, v_ref, ga_ref, log_row_ref, delta_row_ref, dq_in, dk_in, dv_in,
    dq_ref, dk_ref, dv_ref,
    probs, steps,
):
    masks = lane_masks()
    units = [(p, g, slice(N * g, N * g + N)) for p in range(3) for g in range(2)]
    for p, g, lanes in units:
        steps[2 * p + g], probs[2 * p + g] = score(
            stack(q_ref[p, :, lanes] * BF(FACTOR), masks),
            stack(ga_ref[p, :, lanes], masks),
            k_ref[p, :, lanes],
            v_ref[p, :, lanes],
            log_row_ref[p, g],
            delta_row_ref[p, g],
        )
    for p, g, lanes in units:
        dq, dk, dv = multiply(
            stack(q_ref[p, :, lanes] * BF(FACTOR), masks),
            stack(ga_ref[p, :, lanes], masks),
            stack(k_ref[p, :, lanes], masks),
            steps[2 * p + g],
            probs[2 * p + g],
        )
        dq_ref[p, :, lanes] = (dq_in[p, :, lanes] + dq) * FACTOR
        dk_ref[p, :, lanes] = dk_in[p, :, lanes] + dk
        dv_ref[p, :, lanes] = dv_in[p, :, lanes] + dv


def layer_kernel(kept_ref, proj_ref, got_ref, out_ref):
    out_ref[...] = (nn(kept_ref[...], proj_ref[...]) + got_ref[...].astype(F32)).astype(BF)


def finish_kernel(dq_ref, dk_ref, dv_ref, got_ref, q_out, k_out, v_out, stage, made, sems):
    stage[...] = got_ref[...].astype(F32)
    copies = []
    for a, (mine, out) in enumerate(((dq_ref, q_out), (dk_ref, k_out), (dv_ref, v_out))):
        for p in range(3):
            for g in range(2):
                lanes = slice(N * g, N * g + N)
                rows = pl.ds(2 * (3 * a + p) + g, N, stride=SENT)
                made[a, p, :, lanes] = (mine[p, :, lanes] + stage[rows, :]).astype(BF)
        copies.append(pltpu.make_async_copy(made.at[a], out, sems.at[a]))
        copies[-1].start()
    for copy in copies:
        copy.wait()


def shape(*dims, dtype=BF):
    return jax.ShapeDtypeStruct(dims, dtype)


def cost(flops, moved):
    return pl.CostEstimate(flops=flops, bytes_accessed=moved, transcendentals=0)


def exchange(sent, rows):
    sent = sent.reshape(N, rows // 2, 2, N)
    got = lax.all_to_all(sent, "band", split_axis=0, concat_axis=0, tiled=True)
    return got.reshape(N * rows, N)


LINE = (3, N, 256)
TOKENS = (3 * HALF, 1024)
PAIR = (3, 2, N, 256)
ROW = (3, 2, 1, 256)
STAGE = pltpu.VMEM((SENT * N, N), F32)
PACKED = pltpu.VMEM((SENT * N, N), BF)
SQUARE = pltpu.VMEM((N, N), F32)


def call(kernel, ins, outs, scratch, name, params=PARAMS, estimate=None):
    many = len(outs) > 1
    return pl.pallas_call(
        kernel,
        out_shape=tuple(outs) if many else outs[0],
        in_specs=[VMEM] * len(ins),
        out_specs=(VMEM,) * len(outs) if many else VMEM,
        scratch_shapes=scratch,
        compiler_params=params,
        cost_estimate=estimate,
        name=name,
    )(*ins)


def own(*ins):
    outs = [shape(*LINE), shape(*ROW, dtype=F32), shape(*ROW, dtype=F32), shape(*LINE, dtype=F32)]
    return call(own_kernel, ins, outs, [], "own", estimate=cost(LONG, 3000000))


def forward(*ins):
    outs = [shape(MIXED * N, N)] + [shape(6, N, 256)] * 3
    outs += [shape(*LINE, dtype=F32), shape(*LINE), shape(40, N, dtype=F32)]
    return call(forward_kernel, ins, outs, [STAGE, SQUARE, pltpu.VMEM((3, *ROW), F32), pltpu.VMEM((12, N, 256), BF)], "forward")


def backward(*ins):
    row = shape(*ROW, dtype=F32)
    outs = (shape(*LINE, dtype=F32),) * 3 + (shape(SENT * N, N), shape(*TOKENS), pltpu.HBM((3 * HALF, 256), BF))
    places = (VMEM, VMEM, VMEM, HBM, VMEM, HBM, VMEM, VMEM)
    six_rows = pltpu.VMEM((6, 2, 1, 256), F32)
    pairs = pltpu.VMEM((12, N, 256), BF)
    scratch = [pltpu.VMEM((MIXED * N, N), F32), SQUARE, pltpu.VMEM(LINE, BF), six_rows, six_rows, STAGE]
    scratch += [pltpu.VMEM((6, N, 256), BF), pltpu.VMEM((6, N, 256), F32), pairs, pairs, PACKED]
    return pl.pallas_call(
        backward_kernel,
        out_shape=outs + (row, row),
        in_specs=[VMEM] * len(ins),
        out_specs=places,
        scratch_shapes=scratch + [pltpu.VMEM((3 * HALF, 256), BF)] + [pltpu.SemaphoreType.DMA] * 2,
        compiler_params=PARAMS,
        name="backward",
    )(*ins)


def own_rows(*ins):
    pairs = pltpu.VMEM((6, N, 256), BF)
    return pl.pallas_call(
        rows_kernel,
        out_shape=(shape(*LINE, dtype=F32),) * 3,
        in_specs=[VMEM] * len(ins),
        out_specs=(VMEM,) * 3,
        scratch_shapes=[pairs, pairs],
        input_output_aliases={6: 0, 7: 1, 8: 2},
        compiler_params=PARAMS,
        cost_estimate=cost(10**8, 10**5),
        name="own_rows",
    )(*ins)


def finish(*ins):
    return pl.pallas_call(
        finish_kernel,
        out_shape=(shape(*LINE),) * 3,
        in_specs=[VMEM] * 4,
        out_specs=(HBM,) * 3,
        scratch_shapes=[STAGE, pltpu.VMEM((3, *LINE), BF), pltpu.SemaphoreType.DMA((3,))],
        compiler_params=PARAMS,
        name="finish",
    )(*ins)


def pack_lines(*ins):
    return pl.pallas_call(
        pack_lines_kernel,
        out_shape=shape(SENT * N, N),
        in_specs=[HBM] * 3,
        out_specs=HBM,
        scratch_shapes=[
            pltpu.VMEM((3, *LINE), BF),
            STAGE,
            PACKED,
            pltpu.SemaphoreType.DMA((3, 2)),
            pltpu.SemaphoreType.DMA((2,)),
        ],
        compiler_params=ROOMY,
        name="pack_lines",
    )(*ins)


def body(queries, attn_keys, attn_values, out_proj, grad_out, plane_axes):
    swap = [(0, 1), (1, 0)]
    q, k, v = queries[0], attn_keys[0], attn_values[0]

    cotangent = grad_out.reshape(TOKENS)
    other = lax.ppermute(cotangent, "head", swap)
    lines = exchange(pack_lines(q, k, v), SENT)
    ga, top, total, own_out = own(cotangent, other, out_proj, q, k, v)

    sent, q6, k6, v6, near_out, far_out, totals = forward(
        plane_axes, q, k, v, ga, top, total, own_out, lines
    )
    mixed = exchange(sent, MIXED)
    dq, dk, dv, sent, given, kept, log_rows, delta_rows = backward(
        plane_axes, q6, k6, v6, ga, near_out, far_out, totals, out_proj, mixed
    )
    arrived = lax.ppermute(given, "head", swap)
    returned = exchange(sent, SENT)
    dq, dk, dv = own_rows(q, k, v, ga, log_rows, delta_rows, dq, dk, dv)
    layer = call(
        layer_kernel, (kept, out_proj, arrived), [shape(*TOKENS)], [], "layer", estimate=cost(LONG, 1500000)
    )
    dq, dk, dv = finish(dq, dk, dv, returned)
    return layer.reshape(1, 3, HALF, 1024), dq[None], dk[None], dv[None]


def solution(mesh):
    lines = P("band", None, None, "head")
    columns = P("band", None, "head", None)
    return jax.shard_map(
        body,
        mesh=mesh,
        in_specs=(lines, lines, lines, P("head", None), columns, P()),
        out_specs=(columns, lines, lines, lines),
        check_vma=False,
    )
```

```python
import jax
import jax.numpy as jnp
from jax import lax
from jax.experimental import pallas as pl
from jax.experimental.pallas import tpu as pltpu
from jax.sharding import PartitionSpec as P

BF = jnp.bfloat16
F32 = jnp.float32
N = 128
HALF = 64
SENT = 18
MIXED = 14
UNROLL = True
FACTOR = 0.125
LONG = 60 * 10**9
PARAMS = pltpu.CompilerParams(vmem_limit_bytes=48 * 1024 * 1024)
ROOMY = pltpu.CompilerParams(vmem_limit_bytes=60 * 1024 * 1024)
VMEM = pl.BlockSpec(memory_space=pltpu.VMEM)
HBM = pl.BlockSpec(memory_space=pltpu.HBM)


def nt(a, b):
    return lax.dot_general(a, b, (((1,), (1,)), ((), ())), preferred_element_type=F32)


def tn(a, b):
    return lax.dot_general(a, b, (((0,), (0,)), ((), ())), preferred_element_type=F32)


def nn(a, b):
    return lax.dot_general(a, b, (((1,), (0,)), ((), ())), preferred_element_type=F32)


def lane_masks():
    lane = lax.broadcasted_iota(jnp.int32, (N, N), 1)
    first = jnp.where(lane < HALF, 1.0, 0.0)
    return first.astype(BF), (1.0 - first).astype(BF)


def stack(x, masks):
    return jnp.concatenate([x * masks[0], x * masks[1]], axis=0)


def head_sums(product):
    row = lax.broadcasted_iota(jnp.int32, (8, 256), 0)
    lane = lax.broadcasted_iota(jnp.int32, (8, 256), 1)
    pick = jnp.where(lane // HALF == row, 1.0, 0.0).astype(BF)
    high = product.astype(BF)
    low = (product - high.astype(F32)).astype(BF)
    return nt(pick, high) + nt(pick, low)


def partners(axes_ref):
    axes = axes_ref[...]
    axis = [axes[b % 3, b // 3] for b in range(6)]
    found = []
    for b in range(6):
        other = jnp.int32(0)
        for c in range(6):
            if c != b:
                other = other + jnp.where(axis[c] == axis[b], jnp.int32(c), jnp.int32(0))
        found.append(other)
    return found


def planes(step):
    lax.fori_loop(0, 3, lambda p, _: (step(p), 0)[1], 0, unroll=UNROLL)


def tall(x):
    return jnp.concatenate([x[:, :N], x[:, N:]], axis=0)


def wide(rows, r):
    return jnp.concatenate([rows[r : r + 1], rows[r + 1 : r + 2]], axis=1)


def spread(columns, r):
    lane = lax.broadcasted_iota(jnp.int32, (N, N), 1)
    return jnp.where(lane < HALF, columns[:, r : r + 1], columns[:, r + 1 : r + 2])


def pack_lines_kernel(q_ref, k_ref, v_ref, out_ref, held, stage, packed, in_sems, out_sems):
    def arriving(a, ref, h):
        cols = slice(HALF * h, HALF * h + HALF)
        return pltpu.make_async_copy(ref.at[:, cols, :], held.at[a, :, cols, :], in_sems.at[a, h])

    def leaving(h):
        rows = pl.ds(HALF * SENT * h, HALF * SENT)
        return pltpu.make_async_copy(packed.at[rows], out_ref.at[rows], out_sems.at[h])

    inputs = (q_ref, k_ref, v_ref)
    for h in range(2):
        for a, ref in enumerate(inputs):
            arriving(a, ref, h).start()
    for h in range(2):
        cols = slice(HALF * h, HALF * h + HALF)
        for a, ref in enumerate(inputs):
            arriving(a, ref, h).wait()
            for p in range(3):
                for g in range(2):
                    rows = pl.ds(HALF * SENT * h + 2 * (3 * a + p) + g, HALF, stride=SENT)
                    stage[rows, :] = held[a, p, cols, N * g : N * g + N].astype(F32)
        rows = slice(HALF * SENT * h, HALF * SENT * h + HALF * SENT)
        packed[rows, :] = stage[rows, :].astype(BF)
        leaving(h).start()
    for h in range(2):
        leaving(h).wait()


def own_kernel(
    own_ref, other_ref, proj_ref, q_ref, k_ref, v_ref,
    ga_ref, top_ref, sum_ref, out_ref,
):
    me = lax.axis_index("head")
    for ref, side in ((own_ref, me), (other_ref, 1 - me)):
        made = nt(ref[...], proj_ref[...]).astype(BF)
        for p in range(3):
            ga_ref[p, pl.ds(pl.multiple_of(side * HALF, HALF), HALF), :] = made[
                HALF * p : HALF * p + HALF
            ]
    masks = lane_masks()

    def step(p):
        for g in range(2):
            lanes = slice(N * g, N * g + N)
            scores = nt(k_ref[p, :, lanes], stack(q_ref[p, :, lanes] * BF(FACTOR), masks))
            top = jnp.max(scores, axis=0, keepdims=True)
            raised = jnp.exp(scores - top)
            top_ref[p, g] = top
            sum_ref[p, g] = jnp.sum(raised, axis=0, keepdims=True)
            out_ref[p, :, lanes] = tn(tall(raised.astype(BF)), stack(v_ref[p, :, lanes], masks))

    planes(step)


def forward_kernel(
    axes_ref, q_ref, k_ref, v_ref, ga_ref, top_ref, sum_ref, own_ref, got_ref,
    send_ref, q6, k6, v6, near_ref, far_ref, totals_ref,
    stage, parts, rows, probs,
):
    masks = lane_masks()
    stage[...] = got_ref[...].astype(F32)
    for a, (mine, six) in enumerate(((q_ref, q6), (k_ref, k6), (v_ref, v6))):
        for p in range(3):
            six[p] = mine[p]
            for g in range(2):
                lines = pl.ds(2 * (3 * a + p) + g, N, stride=SENT)
                six[3 + p, :, N * g : N * g + N] = stage[lines, :].astype(BF)

    blocks = list(enumerate(partners(axes_ref)))
    for g in range(2):
        lanes = slice(N * g, N * g + N)
        for b, c in blocks:
            p = b % 3
            scores = nt(k6[c, :, lanes], stack(q6[b, :, lanes] * BF(FACTOR), masks))
            top = jnp.max(scores, axis=0, keepdims=True)
            if b < 3:
                top = jnp.maximum(top, top_ref[p, g])
                before = jnp.exp(top_ref[p, g] - top)
            raised = jnp.exp(scores - top)
            total = jnp.sum(raised, axis=0, keepdims=True)
            if b < 3:
                total = total + sum_ref[p, g] * before
            scale = 1.0 / total
            probs[2 * b + g] = (raised * scale).astype(BF)
            rows[b // 3, p, g] = top + jnp.log(total)
            if b < 3:
                rows[2, p, g] = before * scale
    for g in range(2):
        lanes = slice(N * g, N * g + N)
        for b, c in blocks:
            out = tn(tall(probs[2 * b + g]), stack(v6[c, :, lanes], masks))
            if b < 3:
                near_ref[b, :, lanes] = out
            else:
                far_ref[b - 3, :, lanes] = out.astype(BF)
    totals_ref[...] = jnp.zeros((40, N), F32)
    parts[...] = jnp.zeros((N, N), F32)
    for p in range(3):
        for g in range(2):
            for h in range(2):
                r = 4 * p + 2 * g + h
                half = slice(N * h, N * h + N)
                totals_ref[r : r + 1, :] = rows[0, p, g, :, half]
                totals_ref[24 + r : 25 + r, :] = rows[1, p, g, :, half]
                parts[r : r + 1, :] = rows[2, p, g, :, half]
    weights = jnp.transpose(parts[...])
    for p in range(3):
        for g in range(2):
            lanes = slice(N * g, N * g + N)
            near_ref[p, :, lanes] += spread(weights, 4 * p + 2 * g) * own_ref[p, :, lanes]
        totals_ref[12 + 4 * p : 16 + 4 * p, :] = head_sums(
            ga_ref[p].astype(F32) * near_ref[p]
        )[:4]
    left = totals_ref[...]
    for piece in range(3):
        rounded = left.astype(BF).astype(F32)
        parts[40 * piece : 40 * piece + 40, :] = rounded
        left = left - rounded
    stage[pl.ds(12, N, stride=MIXED), :] = jnp.transpose(parts[...])
    stage[pl.ds(13, N, stride=MIXED), :] = jnp.zeros((N, N), F32)
    for p in range(3):
        for g in range(2):
            lanes = slice(N * g, N * g + N)
            stage[pl.ds(2 * p + g, N, stride=MIXED), :] = far_ref[p, :, lanes].astype(F32)
            stage[pl.ds(6 + 2 * p + g, N, stride=MIXED), :] = ga_ref[p, :, lanes].astype(F32)
    send_ref[...] = stage[: MIXED * N, :].astype(BF)


def both_weights(near, far):
    top = jnp.maximum(near, far)
    log_all = top + jnp.log(jnp.exp(near - top) + jnp.exp(far - top))
    return log_all, jnp.exp(near - log_all), jnp.exp(far - log_all)


def score(queries, grads, keys, values, log_all, delta):
    prob = jnp.exp(nt(keys, queries) - log_all)
    return (prob * (nt(values, grads) - delta)).astype(BF), prob.astype(BF)


def multiply(queries, grads, keys, step, prob):
    return tn(tall(step), keys), nn(step, queries), nn(prob, grads)


def backward_kernel(
    axes_ref, q6, k6, v6, ga_ref, near_ref, far_ref, totals_ref, proj_ref, got_ref,
    dq_ref, dk_ref, dv_ref, send_ref, given_ref, kept_ref, log_row_ref, delta_row_ref,
    mixed, parts, att, log_all, delta, stage, ga6, dq6, probs, steps, packed, kept, sem, kept_sem,
):
    masks = lane_masks()
    mixed[...] = got_ref[...].astype(F32)
    parts[...] = jnp.transpose(mixed[pl.ds(12, N, stride=MIXED), :])
    arrived = parts[0:40, :] + (parts[40:80, :] + parts[80:120, :])
    for p in range(3):
        ga6[p] = ga_ref[p]
        for g in range(2):
            ga6[3 + p, :, N * g : N * g + N] = mixed[
                pl.ds(6 + 2 * p + g, N, stride=MIXED), :
            ].astype(BF)
    row_log, row_near, row_far = both_weights(totals_ref[0:12, :], arrived[24:36])
    col_log, col_near, col_far = both_weights(arrived[0:12], totals_ref[24:36, :])
    row_delta = row_near * totals_ref[12:24, :]
    col_delta = col_near * arrived[12:24]
    for p in range(3):
        far_row = jnp.concatenate(
            [mixed[pl.ds(2 * p + g, N, stride=MIXED), :] for g in range(2)], axis=1
        )
        heads = slice(4 * p, 4 * p + 4)
        row_sums = head_sums(ga_ref[p].astype(F32) * far_row)[:4]
        col_sums = head_sums(ga6[3 + p].astype(F32) * far_ref[p].astype(F32))[:4]
        row = row_delta[heads] + row_far[heads] * row_sums
        col = col_delta[heads] + col_far[heads] * col_sums
        for g in range(2):
            log_all[p, g] = wide(row_log, 4 * p + 2 * g)
            log_all[3 + p, g] = wide(col_log, 4 * p + 2 * g)
            delta[p, g] = wide(row, 2 * g)
            delta[3 + p, g] = wide(col, 2 * g)
    parts[0:12, :] = row_near
    parts[12:24, :] = row_far

    cross = list(enumerate(partners(axes_ref)))
    for g in range(2):
        lanes = slice(N * g, N * g + N)
        for c, b in cross:
            steps[2 * c + g], probs[2 * c + g] = score(
                stack(q6[b, :, lanes] * BF(FACTOR), masks),
                stack(ga6[b, :, lanes], masks),
                k6[c, :, lanes],
                v6[c, :, lanes],
                log_all[b, g],
                delta[b, g],
            )
    weights = jnp.transpose(parts[...])
    for p in range(3):
        log_row_ref[p] = log_all[p]
        delta_row_ref[p] = delta[p]
        for g in range(2):
            r = 4 * p + 2 * g
            att[p, :, N * g : N * g + N] = (
                spread(weights, r) * near_ref[p, :, N * g : N * g + N]
                + spread(weights, 12 + r) * mixed[pl.ds(2 * p + g, N, stride=MIXED), :]
            ).astype(BF)
    me = lax.axis_index("head")
    theirs = pl.ds(pl.multiple_of((1 - me) * HALF, HALF), HALF)
    mine = pl.ds(pl.multiple_of(me * HALF, HALF), HALF)
    for p in range(3):
        kept[HALF * p : HALF * p + HALF, :] = att[p, mine, :]
    keeping = pltpu.make_async_copy(kept, kept_ref, kept_sem)
    keeping.start()
    for g in range(2):
        lanes = slice(N * g, N * g + N)
        for c, b in cross:
            dq, dk, dv = multiply(
                stack(q6[b, :, lanes] * BF(FACTOR), masks),
                stack(ga6[b, :, lanes], masks),
                stack(k6[c, :, lanes], masks),
                steps[2 * c + g],
                probs[2 * c + g],
            )
            dq6[b, :, lanes] = dq
            if c < 3:
                dk_ref[c, :, lanes] = dk
                dv_ref[c, :, lanes] = dv
            else:
                stage[pl.ds(2 * c + g, N, stride=SENT), :] = dk
                stage[pl.ds(6 + 2 * c + g, N, stride=SENT), :] = dv
    for p in range(3):
        for g in range(2):
            lanes = slice(N * g, N * g + N)
            stage[pl.ds(2 * p + g, N, stride=SENT), :] = dq6[3 + p, :, lanes] * FACTOR
    packed[...] = stage[...].astype(BF)
    leaving = pltpu.make_async_copy(packed, send_ref, sem)
    leaving.start()

    for p in range(3):
        dq_ref[p] = dq6[p]
    for p in range(3):
        given_ref[HALF * p : HALF * p + HALF, :] = nn(att[p, theirs, :], proj_ref[...]).astype(BF)
    keeping.wait()
    leaving.wait()


def rows_kernel(
    q_ref, k_ref, v_ref, ga_ref, log_row_ref, delta_row_ref, dq_in, dk_in, dv_in,
    dq_ref, dk_ref, dv_ref,
    probs, steps,
):
    masks = lane_masks()
    units = [(p, g, slice(N * g, N * g + N)) for p in range(3) for g in range(2)]
    for p, g, lanes in units:
        steps[2 * p + g], probs[2 * p + g] = score(
            stack(q_ref[p, :, lanes] * BF(FACTOR), masks),
            stack(ga_ref[p, :, lanes], masks),
            k_ref[p, :, lanes],
            v_ref[p, :, lanes],
            log_row_ref[p, g],
            delta_row_ref[p, g],
        )
    for p, g, lanes in units:
        dq, dk, dv = multiply(
            stack(q_ref[p, :, lanes] * BF(FACTOR), masks),
            stack(ga_ref[p, :, lanes], masks),
            stack(k_ref[p, :, lanes], masks),
            steps[2 * p + g],
            probs[2 * p + g],
        )
        dq_ref[p, :, lanes] = (dq_in[p, :, lanes] + dq) * FACTOR
        dk_ref[p, :, lanes] = dk_in[p, :, lanes] + dk
        dv_ref[p, :, lanes] = dv_in[p, :, lanes] + dv


def layer_kernel(kept_ref, proj_ref, got_ref, out_ref):
    out_ref[...] = (nn(kept_ref[...], proj_ref[...]) + got_ref[...].astype(F32)).astype(BF)


def finish_kernel(dq_ref, dk_ref, dv_ref, got_ref, q_out, k_out, v_out, stage, made, sems):
    stage[...] = got_ref[...].astype(F32)
    copies = []
    for a, (mine, out) in enumerate(((dq_ref, q_out), (dk_ref, k_out), (dv_ref, v_out))):
        for p in range(3):
            for g in range(2):
                lanes = slice(N * g, N * g + N)
                rows = pl.ds(2 * (3 * a + p) + g, N, stride=SENT)
                made[a, p, :, lanes] = (mine[p, :, lanes] + stage[rows, :]).astype(BF)
        copies.append(pltpu.make_async_copy(made.at[a], out, sems.at[a]))
        copies[-1].start()
    for copy in copies:
        copy.wait()


def shape(*dims, dtype=BF):
    return jax.ShapeDtypeStruct(dims, dtype)


def cost(flops, moved):
    return pl.CostEstimate(flops=flops, bytes_accessed=moved, transcendentals=0)


def exchange(sent, rows):
    sent = sent.reshape(N, rows // 2, 2, N)
    got = lax.all_to_all(sent, "band", split_axis=0, concat_axis=0, tiled=True)
    return got.reshape(N * rows, N)


LINE = (3, N, 256)
TOKENS = (3 * HALF, 1024)
PAIR = (3, 2, N, 256)
ROW = (3, 2, 1, 256)
STAGE = pltpu.VMEM((SENT * N, N), F32)
PACKED = pltpu.VMEM((SENT * N, N), BF)
SQUARE = pltpu.VMEM((N, N), F32)


def call(kernel, ins, outs, scratch, name, params=PARAMS, estimate=None):
    many = len(outs) > 1
    return pl.pallas_call(
        kernel,
        out_shape=tuple(outs) if many else outs[0],
        in_specs=[VMEM] * len(ins),
        out_specs=(VMEM,) * len(outs) if many else VMEM,
        scratch_shapes=scratch,
        compiler_params=params,
        cost_estimate=estimate,
        name=name,
    )(*ins)


def own(*ins):
    outs = [shape(*LINE), shape(*ROW, dtype=F32), shape(*ROW, dtype=F32), shape(*LINE, dtype=F32)]
    return call(own_kernel, ins, outs, [], "own", estimate=cost(LONG, 3000000))


def forward(*ins):
    outs = [shape(MIXED * N, N)] + [shape(6, N, 256)] * 3
    outs += [shape(*LINE, dtype=F32), shape(*LINE), shape(40, N, dtype=F32)]
    return call(forward_kernel, ins, outs, [STAGE, SQUARE, pltpu.VMEM((3, *ROW), F32), pltpu.VMEM((12, N, 256), BF)], "forward")


def backward(*ins):
    row = shape(*ROW, dtype=F32)
    outs = (shape(*LINE, dtype=F32),) * 3 + (shape(SENT * N, N), shape(*TOKENS), pltpu.HBM((3 * HALF, 256), BF))
    places = (VMEM, VMEM, VMEM, HBM, VMEM, HBM, VMEM, VMEM)
    six_rows = pltpu.VMEM((6, 2, 1, 256), F32)
    pairs = pltpu.VMEM((12, N, 256), BF)
    scratch = [pltpu.VMEM((MIXED * N, N), F32), SQUARE, pltpu.VMEM(LINE, BF), six_rows, six_rows, STAGE]
    scratch += [pltpu.VMEM((6, N, 256), BF), pltpu.VMEM((6, N, 256), F32), pairs, pairs, PACKED]
    return pl.pallas_call(
        backward_kernel,
        out_shape=outs + (row, row),
        in_specs=[VMEM] * len(ins),
        out_specs=places,
        scratch_shapes=scratch + [pltpu.VMEM((3 * HALF, 256), BF)] + [pltpu.SemaphoreType.DMA] * 2,
        compiler_params=PARAMS,
        name="backward",
    )(*ins)


def own_rows(*ins):
    pairs = pltpu.VMEM((6, N, 256), BF)
    return pl.pallas_call(
        rows_kernel,
        out_shape=(shape(*LINE, dtype=F32),) * 3,
        in_specs=[VMEM] * len(ins),
        out_specs=(VMEM,) * 3,
        scratch_shapes=[pairs, pairs],
        input_output_aliases={6: 0, 7: 1, 8: 2},
        compiler_params=PARAMS,
        cost_estimate=cost(10**8, 10**5),
        name="own_rows",
    )(*ins)


def finish(*ins):
    return pl.pallas_call(
        finish_kernel,
        out_shape=(shape(*LINE),) * 3,
        in_specs=[VMEM] * 4,
        out_specs=(HBM,) * 3,
        scratch_shapes=[STAGE, pltpu.VMEM((3, *LINE), BF), pltpu.SemaphoreType.DMA((3,))],
        compiler_params=PARAMS,
        name="finish",
    )(*ins)


def pack_lines(*ins):
    return pl.pallas_call(
        pack_lines_kernel,
        out_shape=shape(SENT * N, N),
        in_specs=[HBM] * 3,
        out_specs=HBM,
        scratch_shapes=[
            pltpu.VMEM((3, *LINE), BF),
            STAGE,
            PACKED,
            pltpu.SemaphoreType.DMA((3, 2)),
            pltpu.SemaphoreType.DMA((2,)),
        ],
        compiler_params=ROOMY,
        name="pack_lines",
    )(*ins)


def body(queries, attn_keys, attn_values, out_proj, grad_out, plane_axes):
    swap = [(0, 1), (1, 0)]
    q, k, v = queries[0], attn_keys[0], attn_values[0]

    cotangent = grad_out.reshape(TOKENS)
    other = lax.ppermute(cotangent, "head", swap)
    lines = exchange(pack_lines(q, k, v), SENT)
    ga, top, total, own_out = own(cotangent, other, out_proj, q, k, v)

    sent, q6, k6, v6, near_out, far_out, totals = forward(
        plane_axes, q, k, v, ga, top, total, own_out, lines
    )
    mixed = exchange(sent, MIXED)
    dq, dk, dv, sent, given, kept, log_rows, delta_rows = backward(
        plane_axes, q6, k6, v6, ga, near_out, far_out, totals, out_proj, mixed
    )
    arrived = lax.ppermute(given, "head", swap)
    returned = exchange(sent, SENT)
    dq, dk, dv = own_rows(q, k, v, ga, log_rows, delta_rows, dq, dk, dv)
    layer = call(
        layer_kernel, (kept, out_proj, arrived), [shape(*TOKENS)], [], "layer", estimate=cost(LONG, 1500000)
    )
    dq, dk, dv = finish(dq, dk, dv, returned)
    return layer.reshape(1, 3, HALF, 1024), dq[None], dk[None], dv[None]


def solution(mesh):
    lines = P("band", None, None, "head")
    columns = P("band", None, "head", None)
    return jax.shard_map(
        body,
        mesh=mesh,
        in_specs=(lines, lines, lines, P("head", None), columns, P()),
        out_specs=(columns, lines, lines, lines),
        check_vma=False,
    )
```

```python
import jax
import jax.numpy as jnp
from jax import lax
from jax.experimental import pallas as pl
from jax.experimental.pallas import tpu as pltpu
from jax.sharding import PartitionSpec as P

BF = jnp.bfloat16
F32 = jnp.float32
N = 128
HALF = 64
SENT = 18
MIXED = 14
UNROLL = True
FACTOR = 0.125
LONG = 60 * 10**9
PARAMS = pltpu.CompilerParams(vmem_limit_bytes=48 * 1024 * 1024)
ROOMY = pltpu.CompilerParams(vmem_limit_bytes=60 * 1024 * 1024)
VMEM = pl.BlockSpec(memory_space=pltpu.VMEM)
HBM = pl.BlockSpec(memory_space=pltpu.HBM)


def nt(a, b):
    return lax.dot_general(a, b, (((1,), (1,)), ((), ())), preferred_element_type=F32)


def tn(a, b):
    return lax.dot_general(a, b, (((0,), (0,)), ((), ())), preferred_element_type=F32)


def nn(a, b):
    return lax.dot_general(a, b, (((1,), (0,)), ((), ())), preferred_element_type=F32)


def lane_masks():
    lane = lax.broadcasted_iota(jnp.int32, (N, N), 1)
    first = jnp.where(lane < HALF, 1.0, 0.0)
    return first.astype(BF), (1.0 - first).astype(BF)


def stack(x, masks):
    return jnp.concatenate([x * masks[0], x * masks[1]], axis=0)


def head_sums(product):
    row = lax.broadcasted_iota(jnp.int32, (8, 256), 0)
    lane = lax.broadcasted_iota(jnp.int32, (8, 256), 1)
    pick = jnp.where(lane // HALF == row, 1.0, 0.0).astype(BF)
    high = product.astype(BF)
    low = (product - high.astype(F32)).astype(BF)
    return nt(pick, high) + nt(pick, low)


def partners(axes_ref):
    axes = axes_ref[...]
    axis = [axes[b % 3, b // 3] for b in range(6)]
    found = []
    for b in range(6):
        other = jnp.int32(0)
        for c in range(6):
            if c != b:
                other = other + jnp.where(axis[c] == axis[b], jnp.int32(c), jnp.int32(0))
        found.append(other)
    return found


def planes(step):
    lax.fori_loop(0, 3, lambda p, _: (step(p), 0)[1], 0, unroll=UNROLL)


def tall(x):
    return jnp.concatenate([x[:, :N], x[:, N:]], axis=0)


def wide(rows, r):
    return jnp.concatenate([rows[r : r + 1], rows[r + 1 : r + 2]], axis=1)


def spread(columns, r):
    lane = lax.broadcasted_iota(jnp.int32, (N, N), 1)
    return jnp.where(lane < HALF, columns[:, r : r + 1], columns[:, r + 1 : r + 2])


def pack_lines_kernel(q_ref, k_ref, v_ref, out_ref, held, stage, packed, in_sems, out_sems):
    def arriving(a, ref, h):
        cols = slice(HALF * h, HALF * h + HALF)
        return pltpu.make_async_copy(ref.at[:, cols, :], held.at[a, :, cols, :], in_sems.at[a, h])

    def leaving(h):
        rows = pl.ds(HALF * SENT * h, HALF * SENT)
        return pltpu.make_async_copy(packed.at[rows], out_ref.at[rows], out_sems.at[h])

    inputs = (q_ref, k_ref, v_ref)
    for h in range(2):
        for a, ref in enumerate(inputs):
            arriving(a, ref, h).start()
    for h in range(2):
        cols = slice(HALF * h, HALF * h + HALF)
        for a, ref in enumerate(inputs):
            arriving(a, ref, h).wait()
            for p in range(3):
                for g in range(2):
                    rows = pl.ds(HALF * SENT * h + 2 * (3 * a + p) + g, HALF, stride=SENT)
                    stage[rows, :] = held[a, p, cols, N * g : N * g + N].astype(F32)
        rows = slice(HALF * SENT * h, HALF * SENT * h + HALF * SENT)
        packed[rows, :] = stage[rows, :].astype(BF)
        leaving(h).start()
    for h in range(2):
        leaving(h).wait()


def own_kernel(
    own_ref, other_ref, proj_ref, q_ref, k_ref, v_ref,
    ga_ref, top_ref, sum_ref, out_ref,
):
    me = lax.axis_index("head")
    for ref, side in ((own_ref, me), (other_ref, 1 - me)):
        made = nt(ref[...], proj_ref[...]).astype(BF)
        for p in range(3):
            ga_ref[p, pl.ds(pl.multiple_of(side * HALF, HALF), HALF), :] = made[
                HALF * p : HALF * p + HALF
            ]
    masks = lane_masks()

    def step(p):
        for g in range(2):
            lanes = slice(N * g, N * g + N)
            scores = nt(k_ref[p, :, lanes], stack(q_ref[p, :, lanes] * BF(FACTOR), masks))
            top = jnp.max(scores, axis=0, keepdims=True)
            raised = jnp.exp(scores - top)
            top_ref[p, g] = top
            sum_ref[p, g] = jnp.sum(raised, axis=0, keepdims=True)
            out_ref[p, :, lanes] = tn(tall(raised.astype(BF)), stack(v_ref[p, :, lanes], masks))

    planes(step)


def forward_kernel(
    axes_ref, q_ref, k_ref, v_ref, ga_ref, top_ref, sum_ref, own_ref, got_ref,
    send_ref, q6, k6, v6, near_ref, far_ref, totals_ref,
    stage, parts, rows, probs,
):
    masks = lane_masks()
    stage[...] = got_ref[...].astype(F32)
    for a, (mine, six) in enumerate(((q_ref, q6), (k_ref, k6), (v_ref, v6))):
        for p in range(3):
            six[p] = mine[p]
            for g in range(2):
                lines = pl.ds(2 * (3 * a + p) + g, N, stride=SENT)
                six[3 + p, :, N * g : N * g + N] = stage[lines, :].astype(BF)

    blocks = list(enumerate(partners(axes_ref)))[::-1]
    for g in range(2):
        lanes = slice(N * g, N * g + N)
        for b, c in blocks:
            p = b % 3
            scores = nt(k6[c, :, lanes], stack(q6[b, :, lanes] * BF(FACTOR), masks))
            top = jnp.max(scores, axis=0, keepdims=True)
            if b < 3:
                top = jnp.maximum(top, top_ref[p, g])
                before = jnp.exp(top_ref[p, g] - top)
            raised = jnp.exp(scores - top)
            total = jnp.sum(raised, axis=0, keepdims=True)
            if b < 3:
                total = total + sum_ref[p, g] * before
            scale = 1.0 / total
            probs[2 * b + g] = (raised * scale).astype(BF)
            rows[b // 3, p, g] = top + jnp.log(total)
            if b < 3:
                rows[2, p, g] = before * scale
    for g in range(2):
        lanes = slice(N * g, N * g + N)
        for b, c in blocks:
            out = tn(tall(probs[2 * b + g]), stack(v6[c, :, lanes], masks))
            if b < 3:
                near_ref[b, :, lanes] = out
            else:
                far_ref[b - 3, :, lanes] = out.astype(BF)
    totals_ref[...] = jnp.zeros((40, N), F32)
    parts[...] = jnp.zeros((N, N), F32)
    for p in range(3):
        for g in range(2):
            for h in range(2):
                r = 4 * p + 2 * g + h
                half = slice(N * h, N * h + N)
                totals_ref[r : r + 1, :] = rows[0, p, g, :, half]
                totals_ref[24 + r : 25 + r, :] = rows[1, p, g, :, half]
                parts[r : r + 1, :] = rows[2, p, g, :, half]
    weights = jnp.transpose(parts[...])
    for p in range(3):
        for g in range(2):
            lanes = slice(N * g, N * g + N)
            near_ref[p, :, lanes] += spread(weights, 4 * p + 2 * g) * own_ref[p, :, lanes]
        totals_ref[12 + 4 * p : 16 + 4 * p, :] = head_sums(
            ga_ref[p].astype(F32) * near_ref[p]
        )[:4]
    left = totals_ref[...]
    for piece in range(3):
        rounded = left.astype(BF).astype(F32)
        parts[40 * piece : 40 * piece + 40, :] = rounded
        left = left - rounded
    stage[pl.ds(12, N, stride=MIXED), :] = jnp.transpose(parts[...])
    stage[pl.ds(13, N, stride=MIXED), :] = jnp.zeros((N, N), F32)
    for p in range(3):
        for g in range(2):
            lanes = slice(N * g, N * g + N)
            stage[pl.ds(2 * p + g, N, stride=MIXED), :] = far_ref[p, :, lanes].astype(F32)
            stage[pl.ds(6 + 2 * p + g, N, stride=MIXED), :] = ga_ref[p, :, lanes].astype(F32)
    send_ref[...] = stage[: MIXED * N, :].astype(BF)


def both_weights(near, far):
    top = jnp.maximum(near, far)
    log_all = top + jnp.log(jnp.exp(near - top) + jnp.exp(far - top))
    return log_all, jnp.exp(near - log_all), jnp.exp(far - log_all)


def score(queries, grads, keys, values, log_all, delta):
    prob = jnp.exp(nt(keys, queries) - log_all)
    return (prob * (nt(values, grads) - delta)).astype(BF), prob.astype(BF)


def multiply(queries, grads, keys, step, prob):
    return tn(tall(step), keys), nn(step, queries), nn(prob, grads)


def backward_kernel(
    axes_ref, q6, k6, v6, ga_ref, near_ref, far_ref, totals_ref, proj_ref, got_ref,
    dq_ref, dk_ref, dv_ref, send_ref, given_ref, kept_ref, log_row_ref, delta_row_ref,
    mixed, parts, att, log_all, delta, stage, ga6, dq6, probs, steps, packed, kept, sem, kept_sem,
):
    masks = lane_masks()
    mixed[...] = got_ref[...].astype(F32)
    parts[...] = jnp.transpose(mixed[pl.ds(12, N, stride=MIXED), :])
    arrived = parts[0:40, :] + (parts[40:80, :] + parts[80:120, :])
    for p in range(3):
        ga6[p] = ga_ref[p]
        for g in range(2):
            ga6[3 + p, :, N * g : N * g + N] = mixed[
                pl.ds(6 + 2 * p + g, N, stride=MIXED), :
            ].astype(BF)
    row_log, row_near, row_far = both_weights(totals_ref[0:12, :], arrived[24:36])
    col_log, col_near, col_far = both_weights(arrived[0:12], totals_ref[24:36, :])
    row_delta = row_near * totals_ref[12:24, :]
    col_delta = col_near * arrived[12:24]
    for p in range(3):
        far_row = jnp.concatenate(
            [mixed[pl.ds(2 * p + g, N, stride=MIXED), :] for g in range(2)], axis=1
        )
        heads = slice(4 * p, 4 * p + 4)
        row_sums = head_sums(ga_ref[p].astype(F32) * far_row)[:4]
        col_sums = head_sums(ga6[3 + p].astype(F32) * far_ref[p].astype(F32))[:4]
        row = row_delta[heads] + row_far[heads] * row_sums
        col = col_delta[heads] + col_far[heads] * col_sums
        for g in range(2):
            log_all[p, g] = wide(row_log, 4 * p + 2 * g)
            log_all[3 + p, g] = wide(col_log, 4 * p + 2 * g)
            delta[p, g] = wide(row, 2 * g)
            delta[3 + p, g] = wide(col, 2 * g)
    parts[0:12, :] = row_near
    parts[12:24, :] = row_far

    cross = list(enumerate(partners(axes_ref)))
    for g in range(2):
        lanes = slice(N * g, N * g + N)
        for c, b in cross:
            steps[2 * c + g], probs[2 * c + g] = score(
                stack(q6[b, :, lanes] * BF(FACTOR), masks),
                stack(ga6[b, :, lanes], masks),
                k6[c, :, lanes],
                v6[c, :, lanes],
                log_all[b, g],
                delta[b, g],
            )
    for g in range(2):
        lanes = slice(N * g, N * g + N)
        for c, b in cross:
            dq, dk, dv = multiply(
                stack(q6[b, :, lanes] * BF(FACTOR), masks),
                stack(ga6[b, :, lanes], masks),
                stack(k6[c, :, lanes], masks),
                steps[2 * c + g],
                probs[2 * c + g],
            )
            dq6[b, :, lanes] = dq
            if c < 3:
                dk_ref[c, :, lanes] = dk
                dv_ref[c, :, lanes] = dv
            else:
                stage[pl.ds(2 * c + g, N, stride=SENT), :] = dk
                stage[pl.ds(6 + 2 * c + g, N, stride=SENT), :] = dv
    for p in range(3):
        for g in range(2):
            lanes = slice(N * g, N * g + N)
            stage[pl.ds(2 * p + g, N, stride=SENT), :] = dq6[3 + p, :, lanes] * FACTOR
    packed[...] = stage[...].astype(BF)
    leaving = pltpu.make_async_copy(packed, send_ref, sem)
    leaving.start()

    weights = jnp.transpose(parts[...])
    for p in range(3):
        dq_ref[p] = dq6[p]
        log_row_ref[p] = log_all[p]
        delta_row_ref[p] = delta[p]
        for g in range(2):
            r = 4 * p + 2 * g
            att[p, :, N * g : N * g + N] = (
                spread(weights, r) * near_ref[p, :, N * g : N * g + N]
                + spread(weights, 12 + r) * mixed[pl.ds(2 * p + g, N, stride=MIXED), :]
            ).astype(BF)
    me = lax.axis_index("head")
    theirs = pl.ds(pl.multiple_of((1 - me) * HALF, HALF), HALF)
    mine = pl.ds(pl.multiple_of(me * HALF, HALF), HALF)
    for p in range(3):
        kept[HALF * p : HALF * p + HALF, :] = att[p, mine, :]
    keeping = pltpu.make_async_copy(kept, kept_ref, kept_sem)
    keeping.start()
    for p in range(3):
        given_ref[HALF * p : HALF * p + HALF, :] = nn(att[p, theirs, :], proj_ref[...]).astype(BF)
    keeping.wait()
    leaving.wait()


def rows_kernel(
    q_ref, k_ref, v_ref, ga_ref, log_row_ref, delta_row_ref, dq_in, dk_in, dv_in,
    dq_ref, dk_ref, dv_ref,
    probs, steps,
):
    masks = lane_masks()
    units = [(p, g, slice(N * g, N * g + N)) for p in range(3) for g in range(2)]
    for p, g, lanes in units:
        steps[2 * p + g], probs[2 * p + g] = score(
            stack(q_ref[p, :, lanes] * BF(FACTOR), masks),
            stack(ga_ref[p, :, lanes], masks),
            k_ref[p, :, lanes],
            v_ref[p, :, lanes],
            log_row_ref[p, g],
            delta_row_ref[p, g],
        )
    for p, g, lanes in units:
        dq, dk, dv = multiply(
            stack(q_ref[p, :, lanes] * BF(FACTOR), masks),
            stack(ga_ref[p, :, lanes], masks),
            stack(k_ref[p, :, lanes], masks),
            steps[2 * p + g],
            probs[2 * p + g],
        )
        dq_ref[p, :, lanes] = (dq_in[p, :, lanes] + dq) * FACTOR
        dk_ref[p, :, lanes] = dk_in[p, :, lanes] + dk
        dv_ref[p, :, lanes] = dv_in[p, :, lanes] + dv


def layer_kernel(kept_ref, proj_ref, got_ref, out_ref):
    out_ref[...] = (nn(kept_ref[...], proj_ref[...]) + got_ref[...].astype(F32)).astype(BF)


def finish_kernel(dq_ref, dk_ref, dv_ref, got_ref, q_out, k_out, v_out, stage, made, sems):
    stage[...] = got_ref[...].astype(F32)
    copies = []
    for a, (mine, out) in enumerate(((dq_ref, q_out), (dk_ref, k_out), (dv_ref, v_out))):
        for p in range(3):
            for g in range(2):
                lanes = slice(N * g, N * g + N)
                rows = pl.ds(2 * (3 * a + p) + g, N, stride=SENT)
                made[a, p, :, lanes] = (mine[p, :, lanes] + stage[rows, :]).astype(BF)
        copies.append(pltpu.make_async_copy(made.at[a], out, sems.at[a]))
        copies[-1].start()
    for copy in copies:
        copy.wait()


def shape(*dims, dtype=BF):
    return jax.ShapeDtypeStruct(dims, dtype)


def cost(flops, moved):
    return pl.CostEstimate(flops=flops, bytes_accessed=moved, transcendentals=0)


def exchange(sent, rows):
    sent = sent.reshape(N, rows // 2, 2, N)
    got = lax.all_to_all(sent, "band", split_axis=0, concat_axis=0, tiled=True)
    return got.reshape(N * rows, N)


LINE = (3, N, 256)
TOKENS = (3 * HALF, 1024)
PAIR = (3, 2, N, 256)
ROW = (3, 2, 1, 256)
STAGE = pltpu.VMEM((SENT * N, N), F32)
PACKED = pltpu.VMEM((SENT * N, N), BF)
SQUARE = pltpu.VMEM((N, N), F32)


def call(kernel, ins, outs, scratch, name, params=PARAMS, estimate=None):
    many = len(outs) > 1
    return pl.pallas_call(
        kernel,
        out_shape=tuple(outs) if many else outs[0],
        in_specs=[VMEM] * len(ins),
        out_specs=(VMEM,) * len(outs) if many else VMEM,
        scratch_shapes=scratch,
        compiler_params=params,
        cost_estimate=estimate,
        name=name,
    )(*ins)


def own(*ins):
    outs = [shape(*LINE), shape(*ROW, dtype=F32), shape(*ROW, dtype=F32), shape(*LINE, dtype=F32)]
    return call(own_kernel, ins, outs, [], "own", estimate=cost(LONG, 3000000))


def forward(*ins):
    outs = [shape(MIXED * N, N)] + [shape(6, N, 256)] * 3
    outs += [shape(*LINE, dtype=F32), shape(*LINE), shape(40, N, dtype=F32)]
    return call(forward_kernel, ins, outs, [STAGE, SQUARE, pltpu.VMEM((3, *ROW), F32), pltpu.VMEM((12, N, 256), BF)], "forward")


def backward(*ins):
    row = shape(*ROW, dtype=F32)
    outs = (shape(*LINE, dtype=F32),) * 3 + (shape(SENT * N, N), shape(*TOKENS), pltpu.HBM((3 * HALF, 256), BF))
    places = (VMEM, VMEM, VMEM, HBM, VMEM, HBM, VMEM, VMEM)
    six_rows = pltpu.VMEM((6, 2, 1, 256), F32)
    pairs = pltpu.VMEM((12, N, 256), BF)
    scratch = [pltpu.VMEM((MIXED * N, N), F32), SQUARE, pltpu.VMEM(LINE, BF), six_rows, six_rows, STAGE]
    scratch += [pltpu.VMEM((6, N, 256), BF), pltpu.VMEM((6, N, 256), F32), pairs, pairs, PACKED]
    return pl.pallas_call(
        backward_kernel,
        out_shape=outs + (row, row),
        in_specs=[VMEM] * len(ins),
        out_specs=places,
        scratch_shapes=scratch + [pltpu.VMEM((3 * HALF, 256), BF)] + [pltpu.SemaphoreType.DMA] * 2,
        compiler_params=PARAMS,
        name="backward",
    )(*ins)


def own_rows(*ins):
    pairs = pltpu.VMEM((6, N, 256), BF)
    return pl.pallas_call(
        rows_kernel,
        out_shape=(shape(*LINE, dtype=F32),) * 3,
        in_specs=[VMEM] * len(ins),
        out_specs=(VMEM,) * 3,
        scratch_shapes=[pairs, pairs],
        input_output_aliases={6: 0, 7: 1, 8: 2},
        compiler_params=PARAMS,
        cost_estimate=cost(10**8, 10**5),
        name="own_rows",
    )(*ins)


def finish(*ins):
    return pl.pallas_call(
        finish_kernel,
        out_shape=(shape(*LINE),) * 3,
        in_specs=[VMEM] * 4,
        out_specs=(HBM,) * 3,
        scratch_shapes=[STAGE, pltpu.VMEM((3, *LINE), BF), pltpu.SemaphoreType.DMA((3,))],
        compiler_params=PARAMS,
        name="finish",
    )(*ins)


def pack_lines(*ins):
    return pl.pallas_call(
        pack_lines_kernel,
        out_shape=shape(SENT * N, N),
        in_specs=[HBM] * 3,
        out_specs=HBM,
        scratch_shapes=[
            pltpu.VMEM((3, *LINE), BF),
            STAGE,
            PACKED,
            pltpu.SemaphoreType.DMA((3, 2)),
            pltpu.SemaphoreType.DMA((2,)),
        ],
        compiler_params=ROOMY,
        name="pack_lines",
    )(*ins)


def body(queries, attn_keys, attn_values, out_proj, grad_out, plane_axes):
    swap = [(0, 1), (1, 0)]
    q, k, v = queries[0], attn_keys[0], attn_values[0]

    cotangent = grad_out.reshape(TOKENS)
    packed = pack_lines(q, k, v)
    cotangent, packed = lax.optimization_barrier((cotangent, packed))
    other = lax.ppermute(cotangent, "head", swap)
    lines = exchange(packed, SENT)
    ga, top, total, own_out = own(cotangent, other, out_proj, q, k, v)

    sent, q6, k6, v6, near_out, far_out, totals = forward(
        plane_axes, q, k, v, ga, top, total, own_out, lines
    )
    mixed = exchange(sent, MIXED)
    dq, dk, dv, sent, given, kept, log_rows, delta_rows = backward(
        plane_axes, q6, k6, v6, ga, near_out, far_out, totals, out_proj, mixed
    )
    arrived = lax.ppermute(given, "head", swap)
    returned = exchange(sent, SENT)
    dq, dk, dv = own_rows(q, k, v, ga, log_rows, delta_rows, dq, dk, dv)
    layer = call(
        layer_kernel, (kept, out_proj, arrived), [shape(*TOKENS)], [], "layer", estimate=cost(LONG, 1500000)
    )
    dq, dk, dv = finish(dq, dk, dv, returned)
    return layer.reshape(1, 3, HALF, 1024), dq[None], dk[None], dv[None]


def solution(mesh):
    lines = P("band", None, None, "head")
    columns = P("band", None, "head", None)
    return jax.shard_map(
        body,
        mesh=mesh,
        in_specs=(lines, lines, lines, P("head", None), columns, P()),
        out_specs=(columns, lines, lines, lines),
        check_vma=False,
    )
```
